32 devices in a mesh: groups: 2 (over x), dom: 16 (over z, y, core).
Axes of the slice: x: 2, y: 2, z: 4, core: 2. Of those that a mesh axis runs over, the one named last changes fastest.
Arguments:
- thickness: float32 [16, 8192], P(None, ('groups', 'dom')), parts along dimension 1, may hold values from 1 to 2
- tracers: float32 [3, 16, 8192], P(None, None, ('groups', 'dom')), parts along dimension 2, may hold values from 0 to 1
- velocity: float32 [2, 16, 8192], P(None, None, ('groups', 'dom')), parts along dimension 2, may hold values from -0.05 to 0.05
- max_level: int32 [7552], P('dom'), may hold values from 0 to 16, as said below
- cells_on_cell: int32 [6, 7552], P(None, 'dom'), may hold values from 0 to 472, as said below
- peer_ids: int32 [16, 8], P('dom'), may hold values from 0 to 15, as said below
- send_ids: int32 [16, 8, 48], P('dom'), may hold values from 0 to 255, as said below
- recv_pos: int32 [16, 8, 48], P('dom'), may hold values from 256 to 472, as said below
Outputs:
- new_thickness: float32 [16, 8192], P(None, ('groups', 'dom')), parts along dimension 1
- new_tracers: float32 [3, 16, 8192], P(None, None, ('groups', 'dom')), parts along dimension 2
The draws below stay inside these ranges and needn't reach their ends.
There are 2 independent parts, one for each index of `groups`. The reference program is written for one: setup_inputs(seed, part) draws one part's arguments, and reference() takes and returns one part's arrays. A program takes and returns all parts, laid end to end along the dimension named above; an argument that names none is the same for every part. Nothing has to cross between parts.
Inputs may be any that keep to these rules, and one draw needn't show every extreme that they name: Layers below max_level are ocean; 0 marks land. Owned cells come first, then halo cells cycle by cycle; a halo cell carries the value of the cell it copies. `cells_on_cell`: entry j names the neighbour in the direction at j * 60 degrees, as a local id; 472 where the neighbour lies beyond the third cycle. Halo positions run from 256, cycle 1 first, then cycles 2 and 3. `peer_ids`: the peers of partition i are i + 1, i - 1, i + 3, i - 3, i + 4, i - 4, i + 5, i - 5, modulo 16, each once, in an order that varies by partition. `send_ids`: owned local ids that partition i sends to peer_ids[i, t], cycle 1 cells first, then cycle 2, then cycle 3; a cycle r cell stands within the first r * 16 slots; slots past the list hold 0. `recv_pos`: slot s of row t: where the s-th cell that peer_ids[i, t] sends to i lands; 472 past the list.
All inputs are finite; a program needn't handle non-finite values.
Results may differ from the reference program's by a relative error of at most 0.0003.
Values sent between devices are 32-bit elements; how exact they have to be, the bound alone decides.
A program may use at most 64 MiB of HBM per device.

```python
import math
import jax
import jax.numpy as jnp
import numpy as np
from jax import lax

NLEV = 16
TX = 16
TY = 16
PGX = 4
PARTITIONS = 16
CELLS_DEV = 256
HALO = 216
LOCAL = 472
SLOT = 48
CELLS = 4096


HEX_EVEN = ((1, 0), (0, 1), (-1, 1), (-1, 0), (-1, -1), (0, -1))


HEX_ODD = ((1, 0), (1, 1), (0, 1), (-1, 0), (0, -1), (1, -1))


OFFSET_PAIRS = ((1, 0), (-1, 0), (-1, 1), (0, 1), (1, 1), (1, -1), (0, -1), (-1, -1))


OPPOSITE = (1, 0, 5, 6, 7, 2, 3, 4)


def window_layout():
    span_x = TX + 6
    span_y = TY + 6
    window_size = span_x * span_y
    grid_y, grid_x = np.meshgrid(np.arange(span_y) - 3, np.arange(span_x) - 3, indexing='ij')
    delta_x = grid_x.reshape(-1)
    delta_y = grid_y.reshape(-1)
    odd_rows = delta_y % 2 == 1
    neighbour_win = np.full((6, window_size), -1, np.int64)
    for direction in range(6):
        move_x = np.where(odd_rows, HEX_ODD[direction][0], HEX_EVEN[direction][0])
        move_y = np.where(odd_rows, HEX_ODD[direction][1], HEX_EVEN[direction][1])
        target_x = delta_x + move_x
        target_y = delta_y + move_y
        inside = (target_x >= -3) & (target_x < TX + 3) & (target_y >= -3) & (target_y < TY + 3)
        neighbour_win[direction] = np.where(inside, (target_y + 3) * span_x + target_x + 3, -1)
    cycle_level = np.where((delta_x >= 0) & (delta_x < TX) & (delta_y >= 0) & (delta_y < TY), 0, 9)
    for level_step in range(1, 4):
        reached = np.zeros(window_size, bool)
        for direction in range(6):
            links = neighbour_win[direction]
            reached = reached | (links >= 0) & (cycle_level[np.maximum(links, 0)] == level_step - 1)
        cycle_level = np.where((cycle_level == 9) & reached, level_step, cycle_level)
    owner_x = delta_x // TX
    owner_y = delta_y // TY
    canonical = np.mod(delta_y, TY) * TX + np.mod(delta_x, TX)
    window_range = np.arange(window_size)
    tile_cells = window_range[cycle_level == 0]
    tile_win = tile_cells[np.argsort(canonical[tile_cells])]
    halo_win = window_range[(cycle_level >= 1) & (cycle_level <= 3)]
    halo_range = np.arange(halo_win.shape[0])
    members = np.full((8, SLOT), -1, np.int64)
    for offset_index in range(8):
        chosen = halo_range[(owner_x[halo_win] == OFFSET_PAIRS[offset_index][0]) & (owner_y[halo_win] == OFFSET_PAIRS[offset_index][1])]
        members[offset_index, :chosen.shape[0]] = chosen
    owner_shift = owner_y * PGX + owner_x
    return (neighbour_win, cycle_level, owner_shift, canonical, tile_win, halo_win, members)


def mesh_tables(key):
    neighbour_win, cycle_level, owner_shift, canonical, tile_win, halo_win, members = window_layout()
    partitions = PARTITIONS
    shift_values = np.array([pair[1] * PGX + pair[0] for pair in OFFSET_PAIRS], np.int32)
    part_rows = jnp.arange(partitions, dtype=jnp.int32)[:, None]
    own_keys = jax.random.split(jax.random.fold_in(key, 11), partitions)
    own_local = jax.vmap(lambda sub_key: jax.random.permutation(sub_key, CELLS_DEV))(own_keys).astype(jnp.int32)
    own_local = jnp.where(own_local == CELLS_DEV - 1, own_local[:, :1], own_local)
    own_local = own_local.at[:, 0].set(CELLS_DEV - 1)
    halo_keys = jax.random.split(jax.random.fold_in(key, 12), partitions)
    halo_rand = jax.vmap(lambda sub_key: jax.random.permutation(sub_key, HALO))(halo_keys).astype(jnp.int32)
    cycle_of_halo = jnp.asarray(cycle_level[halo_win], jnp.int32)
    composite = cycle_of_halo[None, :] * HALO + halo_rand
    halo_pos = (CELLS_DEV + jnp.argsort(jnp.argsort(composite, axis=1), axis=1)).astype(jnp.int32)
    window_size = cycle_level.shape[0]
    local_of_win = jnp.full((partitions, window_size), LOCAL, jnp.int32)
    local_of_win = local_of_win.at[:, tile_win].set(own_local)
    local_of_win = local_of_win.at[:, halo_win].set(halo_pos)
    linked = jnp.where(jnp.asarray(neighbour_win >= 0)[None], local_of_win[:, np.maximum(neighbour_win, 0)], LOCAL)
    sources = np.concatenate([tile_win, halo_win])
    targets = jnp.concatenate([own_local, halo_pos], axis=1)

    def place_one(target_row, linked_row):
        return jnp.zeros((6, LOCAL), jnp.int32).at[:, target_row].set(linked_row[:, sources])
    placed = jax.vmap(place_one)(targets, linked)
    cells_on_cell = jnp.transpose(placed, (1, 0, 2)).reshape(6, partitions * LOCAL)
    level_key = jax.random.fold_in(key, 13)
    shallow = jax.random.randint(jax.random.fold_in(level_key, 1), (partitions, 1), 1, NLEV + 1)
    levels = jax.random.randint(jax.random.fold_in(level_key, 2), (partitions, CELLS_DEV), shallow, NLEV + 1)
    land = jax.random.randint(jax.random.fold_in(level_key, 3), (partitions, CELLS_DEV), 0, 8) == 0
    levels = jnp.where(land, 0, levels).astype(jnp.int32)
    levels = levels.at[:, 0].set(NLEV).at[:, 1].set(0)
    owner_part = (part_rows + jnp.asarray(owner_shift[sources], jnp.int32)[None, :]) % partitions
    level_local = jnp.zeros((partitions, LOCAL), jnp.int32).at[part_rows, targets].set(levels[owner_part, jnp.asarray(canonical[sources], jnp.int32)[None, :]])
    slot_keys = jax.random.split(jax.random.fold_in(key, 14), partitions)
    slot_order = jax.vmap(lambda sub_key: jax.random.permutation(sub_key, 8))(slot_keys).astype(jnp.int32)
    slot_of = jnp.argsort(slot_order, axis=1).astype(jnp.int32)
    shift_table = jnp.asarray(shift_values)
    peer_ids = ((part_rows + shift_table[slot_order]) % partitions).astype(jnp.int32)
    pad_keys = jnp.asarray(LOCAL + 1 + np.arange(SLOT), jnp.int32)
    member_pos = jnp.where(jnp.asarray(members >= 0)[None], halo_pos[:, np.maximum(members, 0)], pad_keys[None, None, :])
    sort_order = jnp.argsort(member_pos, axis=2)
    sorted_keys = jnp.take_along_axis(member_pos, sort_order, axis=2)
    sorted_members = jnp.take_along_axis(jnp.broadcast_to(jnp.asarray(members, jnp.int32), (partitions, 8, SLOT)), sort_order, axis=2)
    valid = sorted_members >= 0
    recv_by_offset = jnp.where(valid, sorted_keys, LOCAL).astype(jnp.int32)
    member_canon = jnp.asarray(canonical[halo_win], jnp.int32)[jnp.maximum(sorted_members, 0)]
    senders = (part_rows + shift_table[None, :]) % partitions
    send_by_offset = jnp.where(valid, own_local[senders[:, :, None], member_canon], 0).astype(jnp.int32)
    recv_pos = jnp.zeros((partitions, 8, SLOT), jnp.int32).at[part_rows, slot_of].set(recv_by_offset)
    gathered = send_by_offset[senders, jnp.asarray(OPPOSITE, jnp.int32)[None, :]]
    send_ids = jnp.zeros((partitions, 8, SLOT), jnp.int32).at[part_rows, slot_of].set(gathered)
    return (level_local.reshape(-1), cells_on_cell, peer_ids, send_ids, recv_pos)


def draw_max_level(key, part):
    tables = mesh_tables(key)
    return tables[0]


def draw_cells_on_cell(key, part):
    tables = mesh_tables(key)
    return tables[1]


def draw_peer_ids(key, part):
    tables = mesh_tables(key)
    return tables[2]


def draw_send_ids(key, part):
    tables = mesh_tables(key)
    return tables[3]


def draw_recv_pos(key, part):
    tables = mesh_tables(key)
    return tables[4]


def block_scale(own_key, dims, cuts, low, largest):
    factor_of = 1.0
    for axis_at, shards_of in cuts:
        heights = jax.random.uniform(jax.random.fold_in(jax.random.fold_in(own_key, 6), axis_at), (shards_of,), jnp.float32, low / len(cuts), largest / len(cuts))
        factor_of = factor_of * jnp.repeat(jnp.exp(heights), dims[axis_at] // shards_of).reshape((-1,) + (1,) * (len(dims) - 1 - axis_at))
    return factor_of


def setup_inputs(seed: int = 0, part: int = 0) -> dict:
    seeds = jax.random.split(jax.random.key(seed), 9)
    part_keys = jax.random.split(jax.random.fold_in(seeds[8], part), 9)
    return {
        "thickness": jnp.clip(1.0 + 1.0 * jax.random.uniform(part_keys[0], (NLEV, CELLS), jnp.float32) ** block_scale(part_keys[0], (NLEV, CELLS), ((1, 16),), -0.2, 0.2), 1.0, 2.0),
        "tracers": jnp.clip(1.0 * jax.random.uniform(part_keys[1], (3, NLEV, CELLS), jnp.float32) ** block_scale(part_keys[1], (3, NLEV, CELLS), ((2, 16),), -0.2, 0.2), 0.0, 1.0),
        "velocity": jnp.clip(jax.random.uniform(part_keys[2], (2, NLEV, CELLS), jnp.float32, -0.05, 0.05) * block_scale(part_keys[2], (2, NLEV, CELLS), ((2, 16),), -0.4, 0.0), -0.05, 0.05),
        "max_level": draw_max_level(jax.random.fold_in(seeds[8], 71), part),
        "cells_on_cell": draw_cells_on_cell(jax.random.fold_in(seeds[8], 71), part),
        "peer_ids": draw_peer_ids(jax.random.fold_in(seeds[8], 71), part),
        "send_ids": draw_send_ids(jax.random.fold_in(seeds[8], 71), part),
        "recv_pos": draw_recv_pos(jax.random.fold_in(seeds[8], 71), part),
    }


THIRD_ORDER = 0.25
LIMIT_FLOOR = 1e-10


def neighbours_of(values, indices):
    return jnp.take(values, indices, axis=-1, mode="fill", fill_value=0)


def curvature_of(active, mixing, neighbour_table):
    running = jnp.zeros_like(mixing)
    for direction in range(6):
        indices = neighbour_table[direction]
        opened = active * neighbours_of(active, indices)
        running = running + opened[None] * (neighbours_of(mixing, indices) - mixing)
    return running


def edge_terms(direction, indices, used_cells, active, depth_h, speed_x, speed_y, mixing, curvature):
    heading = direction * math.pi / 3.0
    opened = active[:, :used_cells] * neighbours_of(active, indices)
    along = math.cos(heading) * (speed_x[:, :used_cells] + neighbours_of(speed_x, indices))
    across = math.sin(heading) * (speed_y[:, :used_cells] + neighbours_of(speed_y, indices))
    transport = opened * (along + across) * 0.5 * ((depth_h[:, :used_cells] + neighbours_of(depth_h, indices)) * 0.5)
    far_mix = neighbours_of(mixing, indices)
    far_curve = neighbours_of(curvature, indices)
    own_mix = mixing[..., :used_cells]
    own_curve = curvature[..., :used_cells]
    lowflux = jnp.maximum(transport, 0.0)[None] * own_mix + jnp.minimum(transport, 0.0)[None] * far_mix
    highflux = transport[None] * (0.5 * (own_mix + far_mix) - (own_curve + far_curve) / 12.0) + THIRD_ORDER * jnp.abs(transport)[None] * (far_curve - own_curve) / 12.0
    return opened, transport, far_mix, lowflux, highflux - lowflux


def low_order_section(neighbour_table, used_cells, active, depth_h, speed_x, speed_y, mixing):
    curvature = curvature_of(active, mixing, neighbour_table)
    own_mix = mixing[..., :used_cells]
    sum_flow = jnp.zeros_like(depth_h[:, :used_cells])
    sum_low = jnp.zeros_like(own_mix)
    inflow = jnp.zeros_like(own_mix)
    outflow = jnp.zeros_like(own_mix)
    upper_bound = own_mix
    lower_bound = own_mix
    anti_terms = []
    for direction in range(6):
        opened, transport, far_mix, lowflux, anti_flux = edge_terms(direction, neighbour_table[direction, :used_cells], used_cells, active, depth_h, speed_x, speed_y, mixing, curvature)
        sum_flow = sum_flow + transport
        sum_low = sum_low + lowflux
        reached = jnp.where(opened[None] > 0, far_mix, own_mix)
        upper_bound = jnp.maximum(upper_bound, reached)
        lower_bound = jnp.minimum(lower_bound, reached)
        inflow = inflow + jnp.maximum(-anti_flux, 0.0)
        outflow = outflow + jnp.maximum(anti_flux, 0.0)
        anti_terms.append(anti_flux)
    new_depth = depth_h[:, :used_cells] - sum_flow
    low_mix = (depth_h[:, :used_cells][None] * own_mix - sum_low) / new_depth[None]
    limit_in = jnp.minimum(1.0, (upper_bound - low_mix) * new_depth[None] / (inflow + LIMIT_FLOOR))
    limit_out = jnp.minimum(1.0, (low_mix - lower_bound) * new_depth[None] / (outflow + LIMIT_FLOOR))
    return new_depth, low_mix, limit_in, limit_out, anti_terms


def corrected(neighbour_table, owned_cells, new_depth, low_mix, limit_in, limit_out, anti_terms):
    own_in = limit_in[..., :owned_cells]
    own_out = limit_out[..., :owned_cells]
    running = jnp.zeros_like(low_mix[..., :owned_cells])
    for direction in range(6):
        indices = neighbour_table[direction, :owned_cells]
        anti_flux = anti_terms[direction][..., :owned_cells]
        factor = jnp.where(anti_flux > 0, jnp.minimum(own_out, neighbours_of(limit_in, indices)), jnp.minimum(own_in, neighbours_of(limit_out, indices)))
        running = running + factor * anti_flux
    return low_mix[..., :owned_cells] - running / new_depth[None, :, :owned_cells]


def global_table(cells_on_cell, peer_ids, send_ids, recv_pos):
    partitions = peer_ids.shape[0]
    slot_range = jnp.arange(peer_ids.shape[1], dtype=jnp.int32)
    their_peers = peer_ids[peer_ids]
    part_index = jnp.arange(partitions, dtype=jnp.int32)
    back_slot = jnp.sum(jnp.where(their_peers == part_index[:, None, None], slot_range[None, None, :], 0), axis=2).astype(jnp.int32)
    sent_local = send_ids[peer_ids, back_slot]
    sent_global = peer_ids[:, :, None] * CELLS_DEV + sent_local
    owned_global = jnp.arange(partitions * CELLS_DEV, dtype=jnp.int32).reshape(partitions, CELLS_DEV)
    local_global = jnp.concatenate([owned_global, jnp.zeros((partitions, LOCAL + 1 - CELLS_DEV), jnp.int32)], axis=1)
    row_index = jnp.broadcast_to(part_index[:, None, None], recv_pos.shape)
    local_global = local_global.at[row_index, recv_pos].set(sent_global)
    owned_table = cells_on_cell.reshape(6, partitions, LOCAL)[:, :, :CELLS_DEV]
    mapped = local_global[part_index[None, :, None], owned_table]
    return mapped.reshape(6, partitions * CELLS_DEV).astype(jnp.int32)


def reference(thickness, tracers, velocity, max_level, cells_on_cell, peer_ids, send_ids, recv_pos):
    neighbour_table = global_table(cells_on_cell, peer_ids, send_ids, recv_pos)
    levels = max_level.reshape(peer_ids.shape[0], LOCAL)[:, :CELLS_DEV].reshape(-1)
    layers = thickness.shape[0]
    used_cells = levels.shape[0]
    active = (lax.broadcasted_iota(jnp.int32, (layers, used_cells), 0) < levels[None, :]).astype(jnp.float32)
    new_depth, low_mix, limit_in, limit_out, anti_terms = low_order_section(neighbour_table, used_cells, active, thickness, velocity[0], velocity[1], tracers)
    new_tracers = corrected(neighbour_table, used_cells, new_depth, low_mix, limit_in, limit_out, anti_terms)
    return new_depth, new_tracers
```

```python
import functools
import math

import jax
import jax.numpy as jnp
from jax import lax
from jax.experimental import pallas as pl
from jax.experimental.pallas import tpu as pltpu
from jax.sharding import PartitionSpec as P

PGX = 4
OFFSETS = (PGX + 1, -PGX - 1, PGX, -PGX, PGX - 1, 1 - PGX, 1, -1)
THIRD_ORDER = 0.25
LIMIT_FLOOR = 1e-10
F32 = jnp.float32
BF16 = jnp.bfloat16
SPAN = 16
BLOCK = 8 * SPAN


def dot(a, b):
    return jnp.dot(a, b, preferred_element_type=F32)


def dot_nt(a, b):
    return lax.dot_general(a, b, (((1,), (1,)), ((), ())), preferred_element_type=F32)


def pieces(x):
    hi = x.astype(BF16)
    lo = (x - hi.astype(F32)).astype(BF16)
    return jnp.concatenate([hi, lo], axis=0)


def joined(x):
    half = x.shape[0] // 2
    return x[:half] + x[half:]


def one_hot(a, b):
    return jnp.where(a == b, 1.0, 0.0).astype(BF16)


def iota(shape, dim):
    return lax.broadcasted_iota(jnp.int32, shape, dim)


def peer_rows(peer, me, partitions, sign, table):
    o = iota((BLOCK, 8), 0) // SPAN
    offset = jnp.zeros((BLOCK, 8), jnp.int32)
    for at, value in enumerate(OFFSETS):
        offset = jnp.where(o == at, sign * value, offset)
    target = me + offset
    target = jnp.where(target >= partitions, target - partitions, target)
    target = jnp.where(target < 0, target + partitions, target)
    chosen = jnp.where(peer == target, 1.0, 0.0)
    return dot(chosen, table)


def slot_columns(rows, block, width):
    slots = rows.shape[1]
    row = iota((BLOCK, slots), 0) % SPAN
    lane = iota((BLOCK, slots), 1)
    own = jnp.where(lane == row + block * SPAN, rows, 0.0)
    return dot(own, jnp.ones((slots, width), F32))


def edges(h, q, vx, vy, curve, opened, far, far_curve, width):
    layers = h.shape[0]
    curves = [curve[m * layers : (m + 1) * layers] for m in range(3)]
    sum_flow = jnp.zeros_like(h)
    sum_low = [jnp.zeros_like(h) for _ in range(3)]
    inflow = [jnp.zeros_like(h) for _ in range(3)]
    outflow = [jnp.zeros_like(h) for _ in range(3)]
    upper = list(q)
    lower = list(q)
    antis = []
    for j in range(6):
        cols = slice(j * width, (j + 1) * width)
        heading = j * math.pi / 3.0
        part = lambda i: far[i * layers : (i + 1) * layers, cols]
        op = opened[:, cols]
        along = math.cos(heading) * (vx + part(4))
        across = math.sin(heading) * (vy + part(5))
        u = op * (along + across) * 0.5 * ((h + part(3)) * 0.5)
        sum_flow = sum_flow + u
        up = jnp.maximum(u, 0.0)
        un = jnp.minimum(u, 0.0)
        ua = THIRD_ORDER * jnp.abs(u)
        row = []
        for m in range(3):
            qn = part(m)
            ln = far_curve[m * layers : (m + 1) * layers, cols]
            low = up * q[m] + un * qn
            high = u * (0.5 * (q[m] + qn) - (curves[m] + ln) / 12.0) + ua * (ln - curves[m]) / 12.0
            sum_low[m] = sum_low[m] + low
            reached = jnp.where(op > 0, qn, q[m])
            upper[m] = jnp.maximum(upper[m], reached)
            lower[m] = jnp.minimum(lower[m], reached)
            a = high - low
            inflow[m] = inflow[m] + jnp.maximum(-a, 0.0)
            outflow[m] = outflow[m] + jnp.maximum(a, 0.0)
            row.append(a)
        antis.append(row)
    depth = h - sum_flow
    lowq, lim_in, lim_out = [], [], []
    for m in range(3):
        low = (h * q[m] - sum_low[m]) / depth
        lowq.append(low)
        lim_in.append(jnp.minimum(1.0, (upper[m] - low) * depth / (inflow[m] + LIMIT_FLOOR)))
        lim_out.append(jnp.minimum(1.0, (low - lower[m]) * depth / (outflow[m] + LIMIT_FLOOR)))
    return depth, lowq, lim_in, lim_out, antis


def curvature(q, far_q, opened, width):
    layers = opened.shape[0]
    out = []
    for m in range(3):
        rows = slice(m * layers, (m + 1) * layers)
        total = jnp.zeros((layers, width), F32)
        for j in range(6):
            cols = slice(j * width, (j + 1) * width)
            total = total + opened[:, cols] * (far_q[rows, cols] - q[m])
        out.append(total)
    return jnp.concatenate(out, axis=0)


def kernel(
    partitions,
    h_ref,
    q_ref,
    v_ref,
    level_ref,
    coc_ref,
    peer_ref,
    send_ref,
    place_ref,
    depth_ref,
    tracer_ref,
    sent,
    came,
    table,
    g_own,
    g_b0,
    g_b1,
    far_own,
    far_b0,
    send_sem,
    recv_sem,
):
    layers, owned = h_ref.shape
    local = coc_ref.shape[1]
    halo = local - owned
    qrows = 3 * layers
    me = lax.axis_index("dom")
    targets = [lax.rem(me + (offset + partitions), partitions) for offset in OFFSETS]
    barrier = pltpu.get_barrier_semaphore()
    for target in targets:
        pl.semaphore_signal(
            barrier, inc=1, device_id={"dom": target}, device_id_type=pl.DeviceIdType.MESH
        )

    peer = peer_ref[...]
    q = [q_ref[m] for m in range(3)]
    h = h_ref[...]
    vx = v_ref[0]
    vy = v_ref[1]
    fields = jnp.concatenate([q[0], q[1], q[2], h, vx, vy], axis=0)
    fields2 = pieces(fields)
    rows96 = 6 * layers
    blank = jnp.zeros((rows96, owned), BF16)
    edge = jnp.zeros((2 * layers, owned), BF16)
    edge1 = jnp.zeros((layers, owned), BF16)
    hi, lo = fields2[:rows96], fields2[rows96:]
    send_rows = peer_rows(peer, me, partitions, 1, send_ref[0].astype(F32))
    lane = iota((BLOCK, owned), 1).astype(F32)
    picks = [one_hot(slot_columns(send_rows, b, owned), lane) for b in range(3)]
    pay = []
    for b in range(2):
        total = None
        for piece in (hi, lo):
            main = jnp.concatenate([piece, edge], axis=0)
            if b == 0:
                tail = jnp.concatenate([blank, piece[: 2 * layers]], axis=0)
            else:
                tail = jnp.concatenate([blank, piece[2 * layers : qrows], edge1], axis=0)
            term = dot_nt(picks[b], main) + dot_nt(picks[2], tail)
            total = term if total is None else total + term
        pay.append(total)
    for p in range(8):
        sent[p, 0:SPAN] = pay[0][p * SPAN : (p + 1) * SPAN]
        sent[p, SPAN : 2 * SPAN] = pay[1][p * SPAN : (p + 1) * SPAN]
    pl.semaphore_wait(barrier, 8)
    copies = []
    for p in range(8):
        copy = pltpu.make_async_remote_copy(
            src_ref=sent.at[p],
            dst_ref=came.at[p],
            send_sem=send_sem.at[p],
            recv_sem=recv_sem.at[p],
            device_id={"dom": targets[p]},
            device_id_type=pl.DeviceIdType.MESH,
        )
        copy.start()
        copies.append(copy)

    place_rows = peer_rows(peer, me, partitions, -1, (place_ref[0] - owned).astype(F32))
    keys = [slot_columns(place_rows, b, owned) for b in range(3)]
    keys = [jnp.where(key == float(halo), -4096.0, key) for key in keys]
    table[...] = jnp.zeros_like(table)
    table[0:6, 0:halo] = coc_ref[:, owned:local].astype(F32)
    table[8:9, 0:halo] = level_ref[:, owned:local].astype(F32)
    entries = table[...]
    above = jnp.where(entries >= float(owned), 1.0, 0.0)
    parts = jnp.concatenate([above, entries - above * float(owned)], axis=0).astype(BF16)
    width_t = table.shape[1]
    lane_t = iota((BLOCK, width_t), 1).astype(F32)
    found = []
    for b in range(3):
        got = dot_nt(parts, one_hot(keys[b][:, :width_t], lane_t))
        found.append(got[:16] * float(owned) + got[16:])
    own_idx = coc_ref[:, 0:owned].astype(F32)
    own_rows = iota((owned, owned), 0).astype(F32)
    for j in range(6):
        idx = own_idx[j : j + 1]
        cols = slice(j * owned, (j + 1) * owned)
        g_own[0:owned, cols] = one_hot(own_rows, idx)
        g_own[owned : owned + BLOCK, cols] = one_hot(keys[0], idx - float(owned))
        cols = slice(j * BLOCK, (j + 1) * BLOCK)
        idx = found[0][j : j + 1]
        g_b0[0:owned, cols] = one_hot(own_rows[:, :BLOCK], idx)
        for b in range(3):
            rows = slice(owned + b * BLOCK, owned + (b + 1) * BLOCK)
            g_b0[rows, cols] = one_hot(keys[b][:, :BLOCK], idx - float(owned))
        idx = found[1][j : j + 1]
        for b in range(3):
            rows = slice(b * BLOCK, (b + 1) * BLOCK)
            g_b1[rows, cols] = one_hot(keys[b][:, :BLOCK], idx - float(owned))

    lev_own = jnp.broadcast_to(level_ref[:, 0:owned].astype(F32), (layers, owned))
    lev_b = [jnp.broadcast_to(found[b][8:9], (layers, BLOCK)) for b in range(3)]
    lev_all = jnp.concatenate([lev_own] + lev_b, axis=1).astype(BF16)

    def opens(near, far, width):
        deep = jnp.concatenate([near] * 6, axis=1)
        layer = iota((layers, 6 * width), 0).astype(F32)
        return jnp.where(layer < jnp.minimum(deep, far), 1.0, 0.0)

    open_own = opens(lev_own, dot(lev_all[:, : owned + BLOCK], g_own[...]), owned)
    open_b0 = opens(lev_b[0], dot(lev_all, g_b0[...]), BLOCK)
    open_b1 = opens(lev_b[1], dot(lev_all[:, owned:], g_b1[...]), BLOCK)

    far_own[...] = joined(dot(fields2, g_own[0:owned, :]))
    far_b0[...] = joined(dot(fields2, g_b0[0:owned, :]))

    for copy in copies:
        copy.wait_recv()

    got0 = jnp.transpose(came[:, 0:SPAN, :].reshape(BLOCK, 8 * layers))
    got1 = jnp.transpose(came[:, SPAN : 2 * SPAN, :].reshape(BLOCK, 8 * layers))
    f0 = got0[:rows96]
    f1 = got1[:rows96]
    q2 = jnp.concatenate([got0[rows96:], got1[rows96 : rows96 + layers]], axis=0)
    fq = pieces(jnp.concatenate([f0[:qrows], f1[:qrows], q2], axis=1))
    fv = pieces(jnp.concatenate([f0[qrows:], f1[qrows:]], axis=1))
    far_o = far_own[...] + joined(dot(pieces(f0), g_own[owned : owned + BLOCK, :]))
    far_b0q = far_b0[0:qrows] + joined(dot(fq, g_b0[owned:, :]))
    far_b0v = far_b0[qrows:] + joined(dot(fv, g_b0[owned : owned + 2 * BLOCK, :]))
    far_b1q = joined(dot(fq, g_b1[...]))

    def tracers_of(f):
        return [f[m * layers : (m + 1) * layers] for m in range(3)]

    q_b0 = tracers_of(f0)
    l_own = curvature(q, far_o, open_own, owned)
    l_b0 = curvature(q_b0, far_b0q, open_b0, BLOCK)
    l_b1 = curvature(tracers_of(f1), far_b1q, open_b1, BLOCK)
    l_all = pieces(jnp.concatenate([l_own, l_b0, l_b1], axis=1))
    lfar_own = joined(dot(l_all[:, : owned + BLOCK], g_own[...]))
    lfar_b0 = joined(dot(l_all, g_b0[0 : owned + 2 * BLOCK, :]))

    far_b = jnp.concatenate([far_b0q, far_b0v], axis=0)
    h0, vx0, vy0 = (f0[i * layers : (i + 1) * layers] for i in range(3, 6))
    depth, lowq, lim_in, lim_out, antis = edges(
        h, q, vx, vy, l_own, open_own, far_o, lfar_own, owned
    )
    _, _, in0, out0, _ = edges(h0, q_b0, vx0, vy0, l_b0, open_b0, far_b, lfar_b0, BLOCK)
    lims = pieces(
        jnp.concatenate(
            [jnp.concatenate([a, b], axis=1) for a, b in zip(lim_in + lim_out, in0 + out0)], axis=0
        )
    )
    rfar = joined(dot(lims, g_own[...]))
    depth_ref[...] = depth
    for m in range(3):
        total = jnp.zeros_like(depth)
        for j in range(6):
            cols = slice(j * owned, (j + 1) * owned)
            a = antis[j][m]
            far_in = rfar[m * layers : (m + 1) * layers, cols]
            far_out = rfar[(3 + m) * layers : (4 + m) * layers, cols]
            factor = jnp.where(
                a > 0, jnp.minimum(lim_out[m], far_in), jnp.minimum(lim_in[m], far_out)
            )
            total = total + factor * a
        tracer_ref[m] = lowq[m] - total / depth
    for copy in copies:
        copy.wait_send()


def shards(
    partitions, thickness, tracers, velocity, max_level, cells_on_cell, peer_ids, send_ids, recv_pos
):
    layers, owned = thickness.shape
    return tuple(
        pl.pallas_call(
            functools.partial(kernel, partitions),
            out_shape=(
                jax.ShapeDtypeStruct(thickness.shape, F32),
                jax.ShapeDtypeStruct(tracers.shape, F32),
            ),
            in_specs=[pl.BlockSpec(memory_space=pltpu.VMEM)] * 8,
            out_specs=[pl.BlockSpec(memory_space=pltpu.VMEM)] * 2,
            scratch_shapes=[
                pltpu.VMEM((8, 2 * SPAN, 8 * layers), F32),
                pltpu.VMEM((8, 2 * SPAN, 8 * layers), F32),
                pltpu.VMEM((16, owned), F32),
                pltpu.VMEM((owned + BLOCK, 6 * owned), BF16),
                pltpu.VMEM((owned + 3 * BLOCK, 6 * BLOCK), BF16),
                pltpu.VMEM((3 * BLOCK, 6 * BLOCK), BF16),
                pltpu.VMEM((6 * layers, 6 * owned), F32),
                pltpu.VMEM((6 * layers, 6 * BLOCK), F32),
                pltpu.SemaphoreType.DMA((8,)),
                pltpu.SemaphoreType.DMA((8,)),
            ],
            compiler_params=pltpu.CompilerParams(
                collective_id=0, has_side_effects=True, vmem_limit_bytes=40 * 1024 * 1024
            ),
        )(
            thickness,
            tracers,
            velocity,
            max_level.reshape(1, -1),
            cells_on_cell,
            peer_ids,
            send_ids,
            recv_pos,
        )
    )


def solution(mesh):
    return jax.shard_map(
        functools.partial(shards, mesh.shape["dom"]),
        mesh=mesh,
        in_specs=(
            P(None, ("groups", "dom")),
            P(None, None, ("groups", "dom")),
            P(None, None, ("groups", "dom")),
            P("dom"),
            P(None, "dom"),
            P("dom", None),
            P("dom", None, None),
            P("dom", None, None),
        ),
        out_specs=(P(None, ("groups", "dom")), P(None, None, ("groups", "dom"))),
        check_vma=False,
    )
```

```python
import functools
import math

import jax
import jax.numpy as jnp
from jax import lax
from jax.experimental import pallas as pl
from jax.experimental.pallas import tpu as pltpu
from jax.sharding import PartitionSpec as P

PGX = 4
OFFSETS = (PGX + 1, -PGX - 1, PGX, -PGX, PGX - 1, 1 - PGX, 1, -1)
THIRD_ORDER = 0.25
LIMIT_FLOOR = 1e-10
F32 = jnp.float32
BF16 = jnp.bfloat16
SPAN = 16
BLOCK = 8 * SPAN


def dot(a, b):
    return jnp.dot(a, b, preferred_element_type=F32)


def dot_nt(a, b):
    return lax.dot_general(a, b, (((1,), (1,)), ((), ())), preferred_element_type=F32)


def pieces(x):
    hi = x.astype(BF16)
    lo = (x - hi.astype(F32)).astype(BF16)
    return jnp.concatenate([hi, lo], axis=0)


def joined(x):
    half = x.shape[0] // 2
    return x[:half] + x[half:]


def one_hot(a, b):
    return jnp.where(a == b, 1.0, 0.0).astype(BF16)


def iota(shape, dim):
    return lax.broadcasted_iota(jnp.int32, shape, dim)


def peer_rows(peer, me, partitions, sign, table):
    o = iota((BLOCK, 8), 0) // SPAN
    offset = jnp.zeros((BLOCK, 8), jnp.int32)
    for at, value in enumerate(OFFSETS):
        offset = jnp.where(o == at, sign * value, offset)
    target = me + offset
    target = jnp.where(target >= partitions, target - partitions, target)
    target = jnp.where(target < 0, target + partitions, target)
    chosen = jnp.where(peer == target, 1.0, 0.0)
    return dot(chosen, table)


def slot_columns(rows, block, width):
    slots = rows.shape[1]
    row = iota((BLOCK, slots), 0) % SPAN
    lane = iota((BLOCK, slots), 1)
    own = jnp.where(lane == row + block * SPAN, rows, 0.0)
    return dot(own, jnp.ones((slots, width), F32))


def edges(h, q, vx, vy, curve, opened, far, far_curve, width):
    layers = h.shape[0]
    curves = [curve[m * layers : (m + 1) * layers] for m in range(3)]
    sum_flow = jnp.zeros_like(h)
    sum_low = [jnp.zeros_like(h) for _ in range(3)]
    inflow = [jnp.zeros_like(h) for _ in range(3)]
    outflow = [jnp.zeros_like(h) for _ in range(3)]
    upper = list(q)
    lower = list(q)
    antis = []
    for j in range(6):
        cols = slice(j * width, (j + 1) * width)
        heading = j * math.pi / 3.0
        part = lambda i: far[i * layers : (i + 1) * layers, cols]
        op = opened[:, cols]
        along = math.cos(heading) * (vx + part(4))
        across = math.sin(heading) * (vy + part(5))
        u = op * (along + across) * 0.5 * ((h + part(3)) * 0.5)
        sum_flow = sum_flow + u
        up = jnp.maximum(u, 0.0)
        un = jnp.minimum(u, 0.0)
        ua = THIRD_ORDER * jnp.abs(u)
        row = []
        for m in range(3):
            qn = part(m)
            ln = far_curve[m * layers : (m + 1) * layers, cols]
            low = up * q[m] + un * qn
            high = u * (0.5 * (q[m] + qn) - (curves[m] + ln) / 12.0) + ua * (ln - curves[m]) / 12.0
            sum_low[m] = sum_low[m] + low
            reached = jnp.where(op > 0, qn, q[m])
            upper[m] = jnp.maximum(upper[m], reached)
            lower[m] = jnp.minimum(lower[m], reached)
            a = high - low
            inflow[m] = inflow[m] + jnp.maximum(-a, 0.0)
            outflow[m] = outflow[m] + jnp.maximum(a, 0.0)
            row.append(a)
        antis.append(row)
    depth = h - sum_flow
    lowq, lim_in, lim_out = [], [], []
    for m in range(3):
        low = (h * q[m] - sum_low[m]) / depth
        lowq.append(low)
        lim_in.append(jnp.minimum(1.0, (upper[m] - low) * depth / (inflow[m] + LIMIT_FLOOR)))
        lim_out.append(jnp.minimum(1.0, (low - lower[m]) * depth / (outflow[m] + LIMIT_FLOOR)))
    return depth, lowq, lim_in, lim_out, antis


def curvature(q, far_q, opened, width):
    layers = opened.shape[0]
    out = []
    for m in range(3):
        rows = slice(m * layers, (m + 1) * layers)
        total = jnp.zeros((layers, width), F32)
        for j in range(6):
            cols = slice(j * width, (j + 1) * width)
            total = total + opened[:, cols] * (far_q[rows, cols] - q[m])
        out.append(total)
    return jnp.concatenate(out, axis=0)


def kernel(
    partitions,
    h_hbm,
    q_hbm,
    v_hbm,
    level_hbm,
    coc_hbm,
    peer_hbm,
    send_hbm,
    place_hbm,
    depth_ref,
    tracer_ref,
    h_ref,
    q_ref,
    v_ref,
    level_ref,
    coc_ref,
    peer_ref,
    send_ref,
    place_ref,
    load_sem,
    sent,
    came,
    table,
    g_own,
    g_b0,
    g_b1,
    far_own,
    far_b0,
    send_sem,
    recv_sem,
):
    loads = [
        pltpu.make_async_copy(src, dst, load_sem.at[at])
        for at, (src, dst) in enumerate(
            (
                (peer_hbm, peer_ref),
                (send_hbm, send_ref),
                (q_hbm, q_ref),
                (h_hbm, h_ref),
                (v_hbm, v_ref),
                (place_hbm, place_ref),
                (coc_hbm, coc_ref),
                (level_hbm, level_ref),
            )
        )
    ]
    for load in loads:
        load.start()
    layers, owned = h_ref.shape
    local = coc_ref.shape[1]
    halo = local - owned
    qrows = 3 * layers
    me = lax.axis_index("dom")
    targets = [lax.rem(me + (offset + partitions), partitions) for offset in OFFSETS]
    barrier = pltpu.get_barrier_semaphore()
    for target in targets:
        pl.semaphore_signal(
            barrier, inc=1, device_id={"dom": target}, device_id_type=pl.DeviceIdType.MESH
        )

    for load in loads[:5]:
        load.wait()

    peer = peer_ref[...]
    q = [q_ref[m] for m in range(3)]
    h = h_ref[...]
    vx = v_ref[0]
    vy = v_ref[1]
    fields = jnp.concatenate([q[0], q[1], q[2], h, vx, vy], axis=0)
    fields2 = pieces(fields)
    rows96 = 6 * layers
    blank = jnp.zeros((rows96, owned), BF16)
    edge = jnp.zeros((2 * layers, owned), BF16)
    edge1 = jnp.zeros((layers, owned), BF16)
    hi, lo = fields2[:rows96], fields2[rows96:]
    send_rows = peer_rows(peer, me, partitions, 1, send_ref[0].astype(F32))
    lane = iota((BLOCK, owned), 1).astype(F32)
    picks = [one_hot(slot_columns(send_rows, b, owned), lane) for b in range(3)]
    pay = []
    for b in range(2):
        total = None
        for piece in (hi, lo):
            main = jnp.concatenate([piece, edge], axis=0)
            if b == 0:
                tail = jnp.concatenate([blank, piece[: 2 * layers]], axis=0)
            else:
                tail = jnp.concatenate([blank, piece[2 * layers : qrows], edge1], axis=0)
            term = dot_nt(picks[b], main) + dot_nt(picks[2], tail)
            total = term if total is None else total + term
        pay.append(total)
    for p in range(8):
        sent[p, 0:SPAN] = pay[0][p * SPAN : (p + 1) * SPAN]
        sent[p, SPAN : 2 * SPAN] = pay[1][p * SPAN : (p + 1) * SPAN]
    pl.semaphore_wait(barrier, 8)
    copies = []
    for p in range(8):
        copy = pltpu.make_async_remote_copy(
            src_ref=sent.at[p],
            dst_ref=came.at[p],
            send_sem=send_sem.at[p],
            recv_sem=recv_sem.at[p],
            device_id={"dom": targets[p]},
            device_id_type=pl.DeviceIdType.MESH,
        )
        copy.start()
        copies.append(copy)

    for load in loads[5:]:
        load.wait()

    place_rows = peer_rows(peer, me, partitions, -1, (place_ref[0] - owned).astype(F32))
    keys = [slot_columns(place_rows, b, owned) for b in range(3)]
    keys = [jnp.where(key == float(halo), -4096.0, key) for key in keys]
    table[...] = jnp.zeros_like(table)
    table[0:6, 0:halo] = coc_ref[:, owned:local].astype(F32)
    table[8:9, 0:halo] = level_ref[:, owned:local].astype(F32)
    entries = table[...]
    above = jnp.where(entries >= float(owned), 1.0, 0.0)
    parts = jnp.concatenate([above, entries - above * float(owned)], axis=0).astype(BF16)
    width_t = table.shape[1]
    lane_t = iota((BLOCK, width_t), 1).astype(F32)
    found = []
    for b in range(3):
        got = dot_nt(parts, one_hot(keys[b][:, :width_t], lane_t))
        found.append(got[:16] * float(owned) + got[16:])
    own_idx = coc_ref[:, 0:owned].astype(F32)
    own_rows = iota((owned, owned), 0).astype(F32)
    for j in range(6):
        idx = own_idx[j : j + 1]
        cols = slice(j * owned, (j + 1) * owned)
        g_own[0:owned, cols] = one_hot(own_rows, idx)
        g_own[owned : owned + BLOCK, cols] = one_hot(keys[0], idx - float(owned))
        cols = slice(j * BLOCK, (j + 1) * BLOCK)
        idx = found[0][j : j + 1]
        g_b0[0:owned, cols] = one_hot(own_rows[:, :BLOCK], idx)
        for b in range(3):
            rows = slice(owned + b * BLOCK, owned + (b + 1) * BLOCK)
            g_b0[rows, cols] = one_hot(keys[b][:, :BLOCK], idx - float(owned))
        idx = found[1][j : j + 1]
        for b in range(3):
            rows = slice(b * BLOCK, (b + 1) * BLOCK)
            g_b1[rows, cols] = one_hot(keys[b][:, :BLOCK], idx - float(owned))

    lev_own = jnp.broadcast_to(level_ref[:, 0:owned].astype(F32), (layers, owned))
    lev_b = [jnp.broadcast_to(found[b][8:9], (layers, BLOCK)) for b in range(3)]
    lev_all = jnp.concatenate([lev_own] + lev_b, axis=1).astype(BF16)

    def opens(near, far, width):
        deep = jnp.concatenate([near] * 6, axis=1)
        layer = iota((layers, 6 * width), 0).astype(F32)
        return jnp.where(layer < jnp.minimum(deep, far), 1.0, 0.0)

    open_own = opens(lev_own, dot(lev_all[:, : owned + BLOCK], g_own[...]), owned)
    open_b0 = opens(lev_b[0], dot(lev_all, g_b0[...]), BLOCK)
    open_b1 = opens(lev_b[1], dot(lev_all[:, owned:], g_b1[...]), BLOCK)

    far_own[...] = joined(dot(fields2, g_own[0:owned, :]))
    far_b0[...] = joined(dot(fields2, g_b0[0:owned, :]))

    for copy in copies:
        copy.wait_recv()

    got0 = jnp.transpose(came[:, 0:SPAN, :].reshape(BLOCK, 8 * layers))
    got1 = jnp.transpose(came[:, SPAN : 2 * SPAN, :].reshape(BLOCK, 8 * layers))
    f0 = got0[:rows96]
    f1 = got1[:rows96]
    q2 = jnp.concatenate([got0[rows96:], got1[rows96 : rows96 + layers]], axis=0)
    fq = pieces(jnp.concatenate([f0[:qrows], f1[:qrows], q2], axis=1))
    fv = pieces(jnp.concatenate([f0[qrows:], f1[qrows:]], axis=1))
    far_o = far_own[...] + joined(dot(pieces(f0), g_own[owned : owned + BLOCK, :]))
    far_b0q = far_b0[0:qrows] + joined(dot(fq, g_b0[owned:, :]))
    far_b0v = far_b0[qrows:] + joined(dot(fv, g_b0[owned : owned + 2 * BLOCK, :]))
    far_b1q = joined(dot(fq, g_b1[...]))

    def tracers_of(f):
        return [f[m * layers : (m + 1) * layers] for m in range(3)]

    q_b0 = tracers_of(f0)
    l_own = curvature(q, far_o, open_own, owned)
    l_b0 = curvature(q_b0, far_b0q, open_b0, BLOCK)
    l_b1 = curvature(tracers_of(f1), far_b1q, open_b1, BLOCK)
    l_all = pieces(jnp.concatenate([l_own, l_b0, l_b1], axis=1))
    lfar_own = joined(dot(l_all[:, : owned + BLOCK], g_own[...]))
    lfar_b0 = joined(dot(l_all, g_b0[0 : owned + 2 * BLOCK, :]))

    far_b = jnp.concatenate([far_b0q, far_b0v], axis=0)
    h0, vx0, vy0 = (f0[i * layers : (i + 1) * layers] for i in range(3, 6))
    depth, lowq, lim_in, lim_out, antis = edges(
        h, q, vx, vy, l_own, open_own, far_o, lfar_own, owned
    )
    _, _, in0, out0, _ = edges(h0, q_b0, vx0, vy0, l_b0, open_b0, far_b, lfar_b0, BLOCK)
    lims = pieces(
        jnp.concatenate(
            [jnp.concatenate([a, b], axis=1) for a, b in zip(lim_in + lim_out, in0 + out0)], axis=0
        )
    )
    rfar = joined(dot(lims, g_own[...]))
    depth_ref[...] = depth
    for m in range(3):
        total = jnp.zeros_like(depth)
        for j in range(6):
            cols = slice(j * owned, (j + 1) * owned)
            a = antis[j][m]
            far_in = rfar[m * layers : (m + 1) * layers, cols]
            far_out = rfar[(3 + m) * layers : (4 + m) * layers, cols]
            factor = jnp.where(
                a > 0, jnp.minimum(lim_out[m], far_in), jnp.minimum(lim_in[m], far_out)
            )
            total = total + factor * a
        tracer_ref[m] = lowq[m] - total / depth
    for copy in copies:
        copy.wait_send()


def store_kernel(depth_ref, tracer_ref, depth_hbm, tracer_hbm, sem):
    first = pltpu.make_async_copy(tracer_ref, tracer_hbm, sem.at[0])
    second = pltpu.make_async_copy(depth_ref, depth_hbm, sem.at[1])
    first.start()
    second.start()
    first.wait()
    second.wait()


def shards(
    partitions, thickness, tracers, velocity, max_level, cells_on_cell, peer_ids, send_ids, recv_pos
):
    layers, owned = thickness.shape
    args = (
        thickness,
        tracers,
        velocity,
        max_level.reshape(1, -1),
        cells_on_cell,
        peer_ids,
        send_ids,
        recv_pos,
    )
    args = tuple(pltpu.with_memory_space_constraint(arg, pltpu.HBM) for arg in args)
    outs = (
        jax.ShapeDtypeStruct(thickness.shape, F32),
        jax.ShapeDtypeStruct(tracers.shape, F32),
    )
    vmem = pl.BlockSpec(memory_space=pltpu.VMEM)
    hbm = pl.BlockSpec(memory_space=pltpu.HBM)
    results = pl.pallas_call(
        functools.partial(kernel, partitions),
        out_shape=tuple(pltpu.VMEM(out.shape, out.dtype) for out in outs),
        in_specs=[hbm] * 8,
        out_specs=[vmem] * 2,
        scratch_shapes=[pltpu.VMEM(arg.shape, arg.dtype) for arg in args]
        + [
            pltpu.SemaphoreType.DMA((8,)),
            pltpu.VMEM((8, 2 * SPAN, 8 * layers), F32),
            pltpu.VMEM((8, 2 * SPAN, 8 * layers), F32),
            pltpu.VMEM((16, owned), F32),
            pltpu.VMEM((owned + BLOCK, 6 * owned), BF16),
            pltpu.VMEM((owned + 3 * BLOCK, 6 * BLOCK), BF16),
            pltpu.VMEM((3 * BLOCK, 6 * BLOCK), BF16),
            pltpu.VMEM((6 * layers, 6 * owned), F32),
            pltpu.VMEM((6 * layers, 6 * BLOCK), F32),
            pltpu.SemaphoreType.DMA((8,)),
            pltpu.SemaphoreType.DMA((8,)),
        ],
        compiler_params=pltpu.CompilerParams(
            collective_id=0, has_side_effects=True, vmem_limit_bytes=40 * 1024 * 1024
        ),
    )(*args)
    return tuple(
        pl.pallas_call(
            store_kernel,
            out_shape=outs,
            in_specs=[vmem] * 2,
            out_specs=[hbm] * 2,
            scratch_shapes=[pltpu.SemaphoreType.DMA((2,))],
        )(*results)
    )


def solution(mesh):
    return jax.shard_map(
        functools.partial(shards, mesh.shape["dom"]),
        mesh=mesh,
        in_specs=(
            P(None, ("groups", "dom")),
            P(None, None, ("groups", "dom")),
            P(None, None, ("groups", "dom")),
            P("dom"),
            P(None, "dom"),
            P("dom", None),
            P("dom", None, None),
            P("dom", None, None),
        ),
        out_specs=(P(None, ("groups", "dom")), P(None, None, ("groups", "dom"))),
        check_vma=False,
    )
```

```python
import functools
import math

import jax
import jax.numpy as jnp
from jax import lax
from jax.experimental import pallas as pl
from jax.experimental.pallas import tpu as pltpu
from jax.sharding import PartitionSpec as P

PGX = 4
OFFSETS = (PGX + 1, -PGX - 1, PGX, -PGX, PGX - 1, 1 - PGX, 1, -1)
THIRD_ORDER = 0.25
LIMIT_FLOOR = 1e-10
F32 = jnp.float32
BF16 = jnp.bfloat16
SPAN = 16
BLOCK = 8 * SPAN


def dot(a, b):
    return jnp.dot(a, b, preferred_element_type=F32)


def dot_nt(a, b):
    return lax.dot_general(a, b, (((1,), (1,)), ((), ())), preferred_element_type=F32)


def pieces(x):
    hi = x.astype(BF16)
    lo = (x - hi.astype(F32)).astype(BF16)
    return jnp.concatenate([hi, lo], axis=0)


def joined(x):
    half = x.shape[0] // 2
    return x[:half] + x[half:]


def one_hot(a, b):
    return jnp.where(a == b, 1.0, 0.0).astype(BF16)


def iota(shape, dim):
    return lax.broadcasted_iota(jnp.int32, shape, dim)


def peer_rows(peer, me, partitions, sign, table):
    o = iota((BLOCK, 8), 0) // SPAN
    offset = jnp.zeros((BLOCK, 8), jnp.int32)
    for at, value in enumerate(OFFSETS):
        offset = jnp.where(o == at, sign * value, offset)
    target = me + offset
    target = jnp.where(target >= partitions, target - partitions, target)
    target = jnp.where(target < 0, target + partitions, target)
    chosen = jnp.where(peer == target, 1.0, 0.0)
    return dot(chosen, table)


def slot_columns(rows, block, width):
    slots = rows.shape[1]
    row = iota((BLOCK, slots), 0) % SPAN
    lane = iota((BLOCK, slots), 1)
    own = jnp.where(lane == row + block * SPAN, rows, 0.0)
    return dot(own, jnp.ones((slots, width), F32))


def edges(h, q, vx, vy, curve, opened, far, far_curve, width):
    layers = h.shape[0]
    curves = [curve[m * layers : (m + 1) * layers] for m in range(3)]
    sum_flow = jnp.zeros_like(h)
    sum_low = [jnp.zeros_like(h) for _ in range(3)]
    inflow = [jnp.zeros_like(h) for _ in range(3)]
    outflow = [jnp.zeros_like(h) for _ in range(3)]
    upper = list(q)
    lower = list(q)
    antis = []
    for j in range(6):
        cols = slice(j * width, (j + 1) * width)
        heading = j * math.pi / 3.0
        part = lambda i: far[i * layers : (i + 1) * layers, cols]
        op = opened[:, cols]
        along = math.cos(heading) * (vx + part(4))
        across = math.sin(heading) * (vy + part(5))
        u = op * (along + across) * 0.5 * ((h + part(3)) * 0.5)
        sum_flow = sum_flow + u
        up = jnp.maximum(u, 0.0)
        un = jnp.minimum(u, 0.0)
        ua = THIRD_ORDER * jnp.abs(u)
        row = []
        for m in range(3):
            qn = part(m)
            ln = far_curve[m * layers : (m + 1) * layers, cols]
            low = up * q[m] + un * qn
            high = u * (0.5 * (q[m] + qn) - (curves[m] + ln) / 12.0) + ua * (ln - curves[m]) / 12.0
            sum_low[m] = sum_low[m] + low
            reached = jnp.where(op > 0, qn, q[m])
            upper[m] = jnp.maximum(upper[m], reached)
            lower[m] = jnp.minimum(lower[m], reached)
            a = high - low
            inflow[m] = inflow[m] + jnp.maximum(-a, 0.0)
            outflow[m] = outflow[m] + jnp.maximum(a, 0.0)
            row.append(a)
        antis.append(row)
    depth = h - sum_flow
    lowq, lim_in, lim_out = [], [], []
    for m in range(3):
        low = (h * q[m] - sum_low[m]) / depth
        lowq.append(low)
        lim_in.append(jnp.minimum(1.0, (upper[m] - low) * depth / (inflow[m] + LIMIT_FLOOR)))
        lim_out.append(jnp.minimum(1.0, (low - lower[m]) * depth / (outflow[m] + LIMIT_FLOOR)))
    return depth, lowq, lim_in, lim_out, antis


def curvature(q, far_q, opened, width):
    layers = opened.shape[0]
    out = []
    for m in range(3):
        rows = slice(m * layers, (m + 1) * layers)
        total = jnp.zeros((layers, width), F32)
        for j in range(6):
            cols = slice(j * width, (j + 1) * width)
            total = total + opened[:, cols] * (far_q[rows, cols] - q[m])
        out.append(total)
    return jnp.concatenate(out, axis=0)


def kernel(
    partitions,
    h_hbm,
    q_hbm,
    v_hbm,
    level_hbm,
    coc_hbm,
    peer_hbm,
    send_hbm,
    place_hbm,
    depth_ref,
    tracer_ref,
    h_ref,
    q_ref,
    v_ref,
    level_ref,
    coc_ref,
    peer_ref,
    send_ref,
    place_ref,
    load_sem,
    sent,
    came,
    table,
    g_own,
    g_b0,
    g_b1,
    far_own,
    far_b0,
    send_sem,
    recv_sem,
):
    loads = [
        pltpu.make_async_copy(src, dst, load_sem.at[at])
        for at, (src, dst) in enumerate(
            (
                (peer_hbm, peer_ref),
                (send_hbm, send_ref),
                (q_hbm, q_ref),
                (h_hbm, h_ref),
                (v_hbm, v_ref),
                (place_hbm, place_ref),
                (coc_hbm, coc_ref),
                (level_hbm, level_ref),
            )
        )
    ]
    for load in loads:
        load.start()
    layers, owned = h_ref.shape
    local = coc_ref.shape[1]
    halo = local - owned
    qrows = 3 * layers
    me = lax.axis_index("dom")
    targets = [lax.rem(me + (offset + partitions), partitions) for offset in OFFSETS]
    barrier = pltpu.get_barrier_semaphore()
    for target in targets:
        pl.semaphore_signal(
            barrier, inc=1, device_id={"dom": target}, device_id_type=pl.DeviceIdType.MESH
        )

    for load in loads[:5]:
        load.wait()

    peer = peer_ref[...]
    q = [q_ref[m] for m in range(3)]
    h = h_ref[...]
    vx = v_ref[0]
    vy = v_ref[1]
    fields = jnp.concatenate([q[0], q[1], q[2], h, vx, vy], axis=0)
    fields2 = pieces(fields)
    rows96 = 6 * layers
    blank = jnp.zeros((rows96, owned), BF16)
    edge = jnp.zeros((2 * layers, owned), BF16)
    edge1 = jnp.zeros((layers, owned), BF16)
    hi, lo = fields2[:rows96], fields2[rows96:]
    send_rows = peer_rows(peer, me, partitions, 1, send_ref[0].astype(F32))
    lane = iota((BLOCK, owned), 1).astype(F32)
    picks = [one_hot(slot_columns(send_rows, b, owned), lane) for b in range(3)]
    pay = []
    for b in range(2):
        total = None
        for piece in (hi, lo):
            main = jnp.concatenate([piece, edge], axis=0)
            if b == 0:
                tail = jnp.concatenate([blank, piece[: 2 * layers]], axis=0)
            else:
                tail = jnp.concatenate([blank, piece[2 * layers : qrows], edge1], axis=0)
            term = dot_nt(picks[b], main) + dot_nt(picks[2], tail)
            total = term if total is None else total + term
        pay.append(total)
    for p in range(8):
        sent[p, 0:SPAN] = pay[0][p * SPAN : (p + 1) * SPAN]
        sent[p, SPAN : 2 * SPAN] = pay[1][p * SPAN : (p + 1) * SPAN]
    pl.semaphore_wait(barrier, 8)
    copies = []
    for p in range(8):
        copy = pltpu.make_async_remote_copy(
            src_ref=sent.at[p],
            dst_ref=came.at[p],
            send_sem=send_sem.at[p],
            recv_sem=recv_sem.at[p],
            device_id={"dom": targets[p]},
            device_id_type=pl.DeviceIdType.MESH,
        )
        copy.start()
        copies.append(copy)

    for load in loads[5:]:
        load.wait()

    place_rows = peer_rows(peer, me, partitions, -1, (place_ref[0] - owned).astype(F32))
    keys = [slot_columns(place_rows, b, owned) for b in range(3)]
    keys = [jnp.where(key == float(halo), -4096.0, key) for key in keys]
    table[...] = jnp.zeros_like(table)
    table[0:6, 0:halo] = coc_ref[:, owned:local].astype(F32)
    table[8:9, 0:halo] = level_ref[:, owned:local].astype(F32)
    entries = table[...]
    above = jnp.where(entries >= float(owned), 1.0, 0.0)
    parts = jnp.concatenate([above, entries - above * float(owned)], axis=0).astype(BF16)
    width_t = table.shape[1]
    lane_t = iota((BLOCK, width_t), 1).astype(F32)
    found = []
    for b in range(3):
        got = dot_nt(parts, one_hot(keys[b][:, :width_t], lane_t))
        found.append(got[:16] * float(owned) + got[16:])
    own_idx = coc_ref[:, 0:owned].astype(F32)
    own_rows = iota((owned, owned), 0).astype(F32)
    for j in range(6):
        idx = own_idx[j : j + 1]
        cols = slice(j * owned, (j + 1) * owned)
        g_own[0:owned, cols] = one_hot(own_rows, idx)
        g_own[owned : owned + BLOCK, cols] = one_hot(keys[0], idx - float(owned))
        cols = slice(j * BLOCK, (j + 1) * BLOCK)
        idx = found[0][j : j + 1]
        g_b0[0:owned, cols] = one_hot(own_rows[:, :BLOCK], idx)
        for b in range(3):
            rows = slice(owned + b * BLOCK, owned + (b + 1) * BLOCK)
            g_b0[rows, cols] = one_hot(keys[b][:, :BLOCK], idx - float(owned))
        idx = found[1][j : j + 1]
        for b in range(3):
            rows = slice(b * BLOCK, (b + 1) * BLOCK)
            g_b1[rows, cols] = one_hot(keys[b][:, :BLOCK], idx - float(owned))

    lev_own = jnp.broadcast_to(level_ref[:, 0:owned].astype(F32), (layers, owned))
    lev_b = [jnp.broadcast_to(found[b][8:9], (layers, BLOCK)) for b in range(3)]
    lev_all = jnp.concatenate([lev_own] + lev_b, axis=1).astype(BF16)

    def opens(near, far, width):
        deep = jnp.concatenate([near] * 6, axis=1)
        layer = iota((layers, 6 * width), 0).astype(F32)
        return jnp.where(layer < jnp.minimum(deep, far), 1.0, 0.0)

    open_own = opens(lev_own, dot(lev_all[:, : owned + BLOCK], g_own[...]), owned)
    open_b0 = opens(lev_b[0], dot(lev_all, g_b0[...]), BLOCK)
    open_b1 = opens(lev_b[1], dot(lev_all[:, owned:], g_b1[...]), BLOCK)

    far_own[...] = joined(dot(fields2, g_own[0:owned, :]))
    far_b0[...] = joined(dot(fields2, g_b0[0:owned, :]))

    for copy in copies:
        copy.wait_recv()

    got0 = jnp.transpose(came[:, 0:SPAN, :].reshape(BLOCK, 8 * layers))
    got1 = jnp.transpose(came[:, SPAN : 2 * SPAN, :].reshape(BLOCK, 8 * layers))
    f0 = got0[:rows96]
    f1 = got1[:rows96]
    q2 = jnp.concatenate([got0[rows96:], got1[rows96 : rows96 + layers]], axis=0)
    fq = pieces(jnp.concatenate([f0[:qrows], f1[:qrows], q2], axis=1))
    fv = pieces(jnp.concatenate([f0[qrows:], f1[qrows:]], axis=1))
    far_o = far_own[...] + joined(dot(pieces(f0), g_own[owned : owned + BLOCK, :]))
    far_b0q = far_b0[0:qrows] + joined(dot(fq, g_b0[owned:, :]))
    far_b0v = far_b0[qrows:] + joined(dot(fv, g_b0[owned : owned + 2 * BLOCK, :]))
    far_b1q = joined(dot(fq, g_b1[...]))

    def tracers_of(f):
        return [f[m * layers : (m + 1) * layers] for m in range(3)]

    q_b0 = tracers_of(f0)
    l_own = curvature(q, far_o, open_own, owned)
    l_b0 = curvature(q_b0, far_b0q, open_b0, BLOCK)
    l_b1 = curvature(tracers_of(f1), far_b1q, open_b1, BLOCK)
    l_all = pieces(jnp.concatenate([l_own, l_b0, l_b1], axis=1))
    lfar_own = joined(dot(l_all[:, : owned + BLOCK], g_own[...]))
    lfar_b0 = joined(dot(l_all, g_b0[0 : owned + 2 * BLOCK, :]))

    far_b = jnp.concatenate([far_b0q, far_b0v], axis=0)
    h0, vx0, vy0 = (f0[i * layers : (i + 1) * layers] for i in range(3, 6))
    depth, lowq, lim_in, lim_out, antis = edges(
        h, q, vx, vy, l_own, open_own, far_o, lfar_own, owned
    )
    _, _, in0, out0, _ = edges(h0, q_b0, vx0, vy0, l_b0, open_b0, far_b, lfar_b0, BLOCK)
    lims = pieces(
        jnp.concatenate(
            [jnp.concatenate([a, b], axis=1) for a, b in zip(lim_in + lim_out, in0 + out0)], axis=0
        )
    )
    rfar = joined(dot(lims, g_own[...]))
    depth_ref[...] = depth
    for m in range(3):
        total = jnp.zeros_like(depth)
        for j in range(6):
            cols = slice(j * owned, (j + 1) * owned)
            a = antis[j][m]
            far_in = rfar[m * layers : (m + 1) * layers, cols]
            far_out = rfar[(3 + m) * layers : (4 + m) * layers, cols]
            factor = jnp.where(
                a > 0, jnp.minimum(lim_out[m], far_in), jnp.minimum(lim_in[m], far_out)
            )
            total = total + factor * a
        tracer_ref[m] = lowq[m] - total / depth
    for copy in copies:
        copy.wait_send()


def store_kernel(depth_ref, tracer_ref, depth_hbm, tracer_hbm, sem):
    first = pltpu.make_async_copy(tracer_ref, tracer_hbm, sem.at[0])
    second = pltpu.make_async_copy(depth_ref, depth_hbm, sem.at[1])
    first.start()
    second.start()
    first.wait()
    second.wait()


def shards(
    partitions, thickness, tracers, velocity, max_level, cells_on_cell, peer_ids, send_ids, recv_pos
):
    layers, owned = thickness.shape
    args = (
        thickness,
        tracers,
        velocity,
        max_level.reshape(1, -1),
        cells_on_cell,
        peer_ids,
        send_ids,
        recv_pos,
    )
    args = tuple(pltpu.with_memory_space_constraint(arg, pltpu.HBM) for arg in args)
    outs = (
        jax.ShapeDtypeStruct(thickness.shape, F32),
        jax.ShapeDtypeStruct(tracers.shape, F32),
    )
    vmem = pl.BlockSpec(memory_space=pltpu.VMEM)
    hbm = pl.BlockSpec(memory_space=pltpu.HBM)
    results = pl.pallas_call(
        functools.partial(kernel, partitions),
        out_shape=tuple(pltpu.VMEM(out.shape, out.dtype) for out in outs),
        in_specs=[hbm] * 8,
        out_specs=[vmem] * 2,
        scratch_shapes=[pltpu.VMEM(arg.shape, arg.dtype) for arg in args]
        + [
            pltpu.SemaphoreType.DMA((8,)),
            pltpu.VMEM((8, 2 * SPAN, 8 * layers), F32),
            pltpu.VMEM((8, 2 * SPAN, 8 * layers), F32),
            pltpu.VMEM((16, owned), F32),
            pltpu.VMEM((owned + BLOCK, 6 * owned), BF16),
            pltpu.VMEM((owned + 3 * BLOCK, 6 * BLOCK), BF16),
            pltpu.VMEM((3 * BLOCK, 6 * BLOCK), BF16),
            pltpu.VMEM((6 * layers, 6 * owned), F32),
            pltpu.VMEM((6 * layers, 6 * BLOCK), F32),
            pltpu.SemaphoreType.DMA((8,)),
            pltpu.SemaphoreType.DMA((8,)),
        ],
        compiler_params=pltpu.CompilerParams(
            collective_id=0, has_side_effects=True, vmem_limit_bytes=40 * 1024 * 1024
        ),
    )(*args)
    results = [pltpu.with_memory_space_constraint(out, pltpu.VMEM) for out in results]
    return tuple(
        pl.pallas_call(
            store_kernel,
            out_shape=outs,
            in_specs=[vmem] * 2,
            out_specs=[hbm] * 2,
            scratch_shapes=[pltpu.SemaphoreType.DMA((2,))],
            compiler_params=pltpu.CompilerParams(vmem_limit_bytes=2 * 1024 * 1024),
        )(*results)
    )


def solution(mesh):
    return jax.shard_map(
        functools.partial(shards, mesh.shape["dom"]),
        mesh=mesh,
        in_specs=(
            P(None, ("groups", "dom")),
            P(None, None, ("groups", "dom")),
            P(None, None, ("groups", "dom")),
            P("dom"),
            P(None, "dom"),
            P("dom", None),
            P("dom", None, None),
            P("dom", None, None),
        ),
        out_specs=(P(None, ("groups", "dom")), P(None, None, ("groups", "dom"))),
        check_vma=False,
    )
```

```python
import functools
import math

import jax
import jax.numpy as jnp
from jax import lax
from jax.experimental import pallas as pl
from jax.experimental.pallas import tpu as pltpu
from jax.sharding import PartitionSpec as P

PGX = 4
OFFSETS = (1, -1, PGX - 1, 1 - PGX, PGX, -PGX, PGX + 1, -PGX - 1)
THIRD_ORDER = 0.25
LIMIT_FLOOR = 1e-10
F32 = jnp.float32
BF16 = jnp.bfloat16
SPAN = 16
BLOCK = 8 * SPAN


def dot(a, b):
    return jnp.dot(a, b, preferred_element_type=F32)


def dot_nt(a, b):
    return lax.dot_general(a, b, (((1,), (1,)), ((), ())), preferred_element_type=F32)


def pieces(x):
    hi = x.astype(BF16)
    lo = (x - hi.astype(F32)).astype(BF16)
    return jnp.concatenate([hi, lo], axis=0)


def joined(x):
    half = x.shape[0] // 2
    return x[:half] + x[half:]


def one_hot(a, b):
    return jnp.where(a == b, 1.0, 0.0).astype(BF16)


def iota(shape, dim):
    return lax.broadcasted_iota(jnp.int32, shape, dim)


def peer_rows(peer, me, partitions, sign, table):
    o = iota((BLOCK, 8), 0) // SPAN
    offset = jnp.zeros((BLOCK, 8), jnp.int32)
    for at, value in enumerate(OFFSETS):
        offset = jnp.where(o == at, sign * value, offset)
    target = me + offset
    target = jnp.where(target >= partitions, target - partitions, target)
    target = jnp.where(target < 0, target + partitions, target)
    chosen = jnp.where(peer == target, 1.0, 0.0)
    return dot(chosen, table)


def slot_columns(rows, block, width):
    slots = rows.shape[1]
    row = iota((BLOCK, slots), 0) % SPAN
    lane = iota((BLOCK, slots), 1)
    own = jnp.where(lane == row + block * SPAN, rows, 0.0)
    return dot(own, jnp.ones((slots, width), F32))


def edges(h, q, vx, vy, curve, opened, far, far_curve, width):
    layers = h.shape[0]
    curves = [curve[m * layers : (m + 1) * layers] for m in range(3)]
    sum_flow = jnp.zeros_like(h)
    sum_low = [jnp.zeros_like(h) for _ in range(3)]
    inflow = [jnp.zeros_like(h) for _ in range(3)]
    outflow = [jnp.zeros_like(h) for _ in range(3)]
    upper = list(q)
    lower = list(q)
    antis = []
    for j in range(6):
        cols = slice(j * width, (j + 1) * width)
        heading = j * math.pi / 3.0
        part = lambda i: far[i * layers : (i + 1) * layers, cols]
        op = opened[:, cols]
        along = math.cos(heading) * (vx + part(4))
        across = math.sin(heading) * (vy + part(5))
        u = op * (along + across) * 0.5 * ((h + part(3)) * 0.5)
        sum_flow = sum_flow + u
        up = jnp.maximum(u, 0.0)
        un = jnp.minimum(u, 0.0)
        ua = THIRD_ORDER * jnp.abs(u)
        row = []
        for m in range(3):
            qn = part(m)
            ln = far_curve[m * layers : (m + 1) * layers, cols]
            low = up * q[m] + un * qn
            high = u * (0.5 * (q[m] + qn) - (curves[m] + ln) / 12.0) + ua * (ln - curves[m]) / 12.0
            sum_low[m] = sum_low[m] + low
            reached = jnp.where(op > 0, qn, q[m])
            upper[m] = jnp.maximum(upper[m], reached)
            lower[m] = jnp.minimum(lower[m], reached)
            a = high - low
            inflow[m] = inflow[m] + jnp.maximum(-a, 0.0)
            outflow[m] = outflow[m] + jnp.maximum(a, 0.0)
            row.append(a)
        antis.append(row)
    depth = h - sum_flow
    lowq, lim_in, lim_out = [], [], []
    for m in range(3):
        low = (h * q[m] - sum_low[m]) / depth
        lowq.append(low)
        lim_in.append(jnp.minimum(1.0, (upper[m] - low) * depth / (inflow[m] + LIMIT_FLOOR)))
        lim_out.append(jnp.minimum(1.0, (low - lower[m]) * depth / (outflow[m] + LIMIT_FLOOR)))
    return depth, lowq, lim_in, lim_out, antis


def curvature(q, far_q, opened, width):
    layers = opened.shape[0]
    out = []
    for m in range(3):
        rows = slice(m * layers, (m + 1) * layers)
        total = jnp.zeros((layers, width), F32)
        for j in range(6):
            cols = slice(j * width, (j + 1) * width)
            total = total + opened[:, cols] * (far_q[rows, cols] - q[m])
        out.append(total)
    return jnp.concatenate(out, axis=0)


def kernel(
    partitions,
    h_hbm,
    q_hbm,
    v_hbm,
    level_hbm,
    coc_hbm,
    peer_hbm,
    send_hbm,
    place_hbm,
    depth_ref,
    tracer_ref,
    h_ref,
    q_ref,
    v_ref,
    level_ref,
    coc_ref,
    peer_ref,
    send_ref,
    place_ref,
    load_sem,
    sent,
    came,
    table,
    g_own,
    g_b0,
    g_b1,
    far_own,
    far_b0,
    send_sem,
    recv_sem,
):
    layers, owned = h_ref.shape
    local = coc_ref.shape[1]
    halo = local - owned
    qrows = 3 * layers
    me = lax.axis_index("dom")
    targets = [lax.rem(me + (offset + partitions), partitions) for offset in OFFSETS]
    barrier = pltpu.get_barrier_semaphore()
    for target in targets:
        pl.semaphore_signal(
            barrier, inc=1, device_id={"dom": target}, device_id_type=pl.DeviceIdType.MESH
        )

    loads = [
        pltpu.make_async_copy(src, dst, load_sem.at[at])
        for at, (src, dst) in enumerate(
            (
                (peer_hbm, peer_ref),
                (send_hbm, send_ref),
                (q_hbm, q_ref),
                (h_hbm, h_ref),
                (v_hbm, v_ref),
                (place_hbm, place_ref),
                (coc_hbm, coc_ref),
                (level_hbm, level_ref),
            )
        )
    ]
    for load in loads:
        load.start()
    for load in loads[:5]:
        load.wait()

    peer = peer_ref[...]
    q = [q_ref[m] for m in range(3)]
    h = h_ref[...]
    vx = v_ref[0]
    vy = v_ref[1]
    fields = jnp.concatenate([q[0], q[1], q[2], h, vx, vy], axis=0)
    fields2 = pieces(fields)
    rows96 = 6 * layers
    blank = jnp.zeros((rows96, owned), BF16)
    edge = jnp.zeros((2 * layers, owned), BF16)
    edge1 = jnp.zeros((layers, owned), BF16)
    hi, lo = fields2[:rows96], fields2[rows96:]
    send_rows = peer_rows(peer, me, partitions, 1, send_ref[0].astype(F32))
    lane = iota((BLOCK, owned), 1).astype(F32)
    picks = [one_hot(slot_columns(send_rows, b, owned), lane) for b in range(3)]
    pay = []
    for b in range(2):
        total = None
        for piece in (hi, lo):
            main = jnp.concatenate([piece, edge], axis=0)
            if b == 0:
                tail = jnp.concatenate([blank, piece[: 2 * layers]], axis=0)
            else:
                tail = jnp.concatenate([blank, piece[2 * layers : qrows], edge1], axis=0)
            term = dot_nt(picks[b], main) + dot_nt(picks[2], tail)
            total = term if total is None else total + term
        pay.append(total)
    for p in range(8):
        sent[p, 0:SPAN] = pay[0][p * SPAN : (p + 1) * SPAN]
        sent[p, SPAN : 2 * SPAN] = pay[1][p * SPAN : (p + 1) * SPAN]
    pl.semaphore_wait(barrier, 8)
    copies = []
    for p in range(8):
        copy = pltpu.make_async_remote_copy(
            src_ref=sent.at[p],
            dst_ref=came.at[p],
            send_sem=send_sem.at[p],
            recv_sem=recv_sem.at[p],
            device_id={"dom": targets[p]},
            device_id_type=pl.DeviceIdType.MESH,
        )
        copy.start()
        copies.append(copy)

    for load in loads[5:]:
        load.wait()

    place_rows = peer_rows(peer, me, partitions, -1, (place_ref[0] - owned).astype(F32))
    keys = [slot_columns(place_rows, b, owned) for b in range(3)]
    keys = [jnp.where(key == float(halo), -4096.0, key) for key in keys]
    table[...] = jnp.zeros_like(table)
    table[0:6, 0:halo] = coc_ref[:, owned:local].astype(F32)
    table[8:9, 0:halo] = level_ref[:, owned:local].astype(F32)
    entries = table[...]
    above = jnp.where(entries >= float(owned), 1.0, 0.0)
    parts = jnp.concatenate([above, entries - above * float(owned)], axis=0).astype(BF16)
    width_t = table.shape[1]
    lane_t = iota((BLOCK, width_t), 1).astype(F32)
    found = []
    for b in range(3):
        got = dot_nt(parts, one_hot(keys[b][:, :width_t], lane_t))
        found.append(got[:16] * float(owned) + got[16:])
    own_idx = coc_ref[:, 0:owned].astype(F32)
    own_rows = iota((owned, owned), 0).astype(F32)
    for j in range(6):
        idx = own_idx[j : j + 1]
        cols = slice(j * owned, (j + 1) * owned)
        g_own[0:owned, cols] = one_hot(own_rows, idx)
        g_own[owned : owned + BLOCK, cols] = one_hot(keys[0], idx - float(owned))
        cols = slice(j * BLOCK, (j + 1) * BLOCK)
        idx = found[0][j : j + 1]
        g_b0[0:owned, cols] = one_hot(own_rows[:, :BLOCK], idx)
        for b in range(3):
            rows = slice(owned + b * BLOCK, owned + (b + 1) * BLOCK)
            g_b0[rows, cols] = one_hot(keys[b][:, :BLOCK], idx - float(owned))
        idx = found[1][j : j + 1]
        for b in range(3):
            rows = slice(b * BLOCK, (b + 1) * BLOCK)
            g_b1[rows, cols] = one_hot(keys[b][:, :BLOCK], idx - float(owned))

    lev_own = jnp.broadcast_to(level_ref[:, 0:owned].astype(F32), (layers, owned))
    lev_b = [jnp.broadcast_to(found[b][8:9], (layers, BLOCK)) for b in range(3)]
    lev_all = jnp.concatenate([lev_own] + lev_b, axis=1).astype(BF16)

    def opens(near, far, width):
        deep = jnp.concatenate([near] * 6, axis=1)
        layer = iota((layers, 6 * width), 0).astype(F32)
        return jnp.where(layer < jnp.minimum(deep, far), 1.0, 0.0)

    open_own = opens(lev_own, dot(lev_all[:, : owned + BLOCK], g_own[...]), owned)
    open_b0 = opens(lev_b[0], dot(lev_all, g_b0[...]), BLOCK)
    open_b1 = opens(lev_b[1], dot(lev_all[:, owned:], g_b1[...]), BLOCK)

    far_own[...] = joined(dot(fields2, g_own[0:owned, :]))
    far_b0[...] = joined(dot(fields2, g_b0[0:owned, :]))

    for copy in copies:
        copy.wait_recv()

    got0 = jnp.transpose(came[:, 0:SPAN, :].reshape(BLOCK, 8 * layers))
    got1 = jnp.transpose(came[:, SPAN : 2 * SPAN, :].reshape(BLOCK, 8 * layers))
    f0 = got0[:rows96]
    f1 = got1[:rows96]
    q2 = jnp.concatenate([got0[rows96:], got1[rows96 : rows96 + layers]], axis=0)
    fq = pieces(jnp.concatenate([f0[:qrows], f1[:qrows], q2], axis=1))
    fv = pieces(jnp.concatenate([f0[qrows:], f1[qrows:]], axis=1))
    far_o = far_own[...] + joined(dot(pieces(f0), g_own[owned : owned + BLOCK, :]))
    far_b0q = far_b0[0:qrows] + joined(dot(fq, g_b0[owned:, :]))
    far_b0v = far_b0[qrows:] + joined(dot(fv, g_b0[owned : owned + 2 * BLOCK, :]))
    far_b1q = dot(fq[:qrows], g_b1[...])

    def tracers_of(f):
        return [f[m * layers : (m + 1) * layers] for m in range(3)]

    q_b0 = tracers_of(f0)
    l_own = curvature(q, far_o, open_own, owned)
    l_b0 = curvature(q_b0, far_b0q, open_b0, BLOCK)
    l_b1 = curvature(tracers_of(f1), far_b1q, open_b1, BLOCK)
    l_all = jnp.concatenate([l_own, l_b0, l_b1], axis=1).astype(BF16)
    lfar_own = dot(l_all[:, : owned + BLOCK], g_own[...])
    lfar_b0 = dot(l_all, g_b0[0 : owned + 2 * BLOCK, :])

    far_b = jnp.concatenate([far_b0q, far_b0v], axis=0)
    h0, vx0, vy0 = (f0[i * layers : (i + 1) * layers] for i in range(3, 6))
    depth, lowq, lim_in, lim_out, antis = edges(
        h, q, vx, vy, l_own, open_own, far_o, lfar_own, owned
    )
    _, _, in0, out0, _ = edges(h0, q_b0, vx0, vy0, l_b0, open_b0, far_b, lfar_b0, BLOCK)
    lims = jnp.concatenate(
        [jnp.concatenate([a, b], axis=1) for a, b in zip(lim_in + lim_out, in0 + out0)], axis=0
    )
    rfar = dot(lims.astype(BF16), g_own[...])
    depth_ref[...] = depth
    for m in range(3):
        total = jnp.zeros_like(depth)
        for j in range(6):
            cols = slice(j * owned, (j + 1) * owned)
            a = antis[j][m]
            far_in = rfar[m * layers : (m + 1) * layers, cols]
            far_out = rfar[(3 + m) * layers : (4 + m) * layers, cols]
            factor = jnp.where(
                a > 0, jnp.minimum(lim_out[m], far_in), jnp.minimum(lim_in[m], far_out)
            )
            total = total + factor * a
        tracer_ref[m] = lowq[m] - total / depth
    for copy in copies:
        copy.wait_send()


def store_kernel(depth_ref, tracer_ref, depth_hbm, tracer_hbm, sem):
    first = pltpu.make_async_copy(tracer_ref, tracer_hbm, sem.at[0])
    second = pltpu.make_async_copy(depth_ref, depth_hbm, sem.at[1])
    first.start()
    second.start()
    first.wait()
    second.wait()


def shards(
    partitions, thickness, tracers, velocity, max_level, cells_on_cell, peer_ids, send_ids, recv_pos
):
    layers, owned = thickness.shape
    args = (
        thickness,
        tracers,
        velocity,
        max_level.reshape(1, -1),
        cells_on_cell,
        peer_ids,
        send_ids,
        recv_pos,
    )
    args = tuple(pltpu.with_memory_space_constraint(arg, pltpu.HBM) for arg in args)
    outs = (
        jax.ShapeDtypeStruct(thickness.shape, F32),
        jax.ShapeDtypeStruct(tracers.shape, F32),
    )
    vmem = pl.BlockSpec(memory_space=pltpu.VMEM)
    hbm = pl.BlockSpec(memory_space=pltpu.HBM)
    results = pl.pallas_call(
        functools.partial(kernel, partitions),
        out_shape=tuple(pltpu.VMEM(out.shape, out.dtype) for out in outs),
        in_specs=[hbm] * 8,
        out_specs=[vmem] * 2,
        scratch_shapes=[pltpu.VMEM(arg.shape, arg.dtype) for arg in args]
        + [
            pltpu.SemaphoreType.DMA((8,)),
            pltpu.VMEM((8, 2 * SPAN, 8 * layers), F32),
            pltpu.VMEM((8, 2 * SPAN, 8 * layers), F32),
            pltpu.VMEM((16, owned), F32),
            pltpu.VMEM((owned + BLOCK, 6 * owned), BF16),
            pltpu.VMEM((owned + 3 * BLOCK, 6 * BLOCK), BF16),
            pltpu.VMEM((3 * BLOCK, 6 * BLOCK), BF16),
            pltpu.VMEM((6 * layers, 6 * owned), F32),
            pltpu.VMEM((6 * layers, 6 * BLOCK), F32),
            pltpu.SemaphoreType.DMA((8,)),
            pltpu.SemaphoreType.DMA((8,)),
        ],
        compiler_params=pltpu.CompilerParams(
            collective_id=0, has_side_effects=True, vmem_limit_bytes=40 * 1024 * 1024
        ),
    )(*args)
    results = [pltpu.with_memory_space_constraint(out, pltpu.VMEM) for out in results]
    return tuple(
        pl.pallas_call(
            store_kernel,
            out_shape=outs,
            in_specs=[vmem] * 2,
            out_specs=[hbm] * 2,
            scratch_shapes=[pltpu.SemaphoreType.DMA((2,))],
            compiler_params=pltpu.CompilerParams(vmem_limit_bytes=2 * 1024 * 1024),
        )(*results)
    )


def solution(mesh):
    return jax.shard_map(
        functools.partial(shards, mesh.shape["dom"]),
        mesh=mesh,
        in_specs=(
            P(None, ("groups", "dom")),
            P(None, None, ("groups", "dom")),
            P(None, None, ("groups", "dom")),
            P("dom"),
            P(None, "dom"),
            P("dom", None),
            P("dom", None, None),
            P("dom", None, None),
        ),
        out_specs=(P(None, ("groups", "dom")), P(None, None, ("groups", "dom"))),
        check_vma=False,
    )
```

```python
import functools
import math

import jax
import jax.numpy as jnp
from jax import lax
from jax.experimental import pallas as pl
from jax.experimental.pallas import tpu as pltpu
from jax.sharding import PartitionSpec as P

PGX = 4
OFFSETS = (1, -1, PGX - 1, 1 - PGX, PGX, -PGX, PGX + 1, -PGX - 1)
THIRD_ORDER = 0.25
LIMIT_FLOOR = 1e-10
F32 = jnp.float32
BF16 = jnp.bfloat16
SPAN = 16
BLOCK = 8 * SPAN


def dot(a, b):
    return jnp.dot(a, b, preferred_element_type=F32)


def dot_nt(a, b):
    return lax.dot_general(a, b, (((1,), (1,)), ((), ())), preferred_element_type=F32)


def pieces(x):
    hi = x.astype(BF16)
    lo = (x - hi.astype(F32)).astype(BF16)
    return jnp.concatenate([hi, lo], axis=0)


def joined(x):
    half = x.shape[0] // 2
    return x[:half] + x[half:]


def one_hot(a, b):
    return jnp.where(a == b, 1.0, 0.0).astype(BF16)


def iota(shape, dim):
    return lax.broadcasted_iota(jnp.int32, shape, dim)


def peer_rows(peer, me, partitions, sign, table):
    o = iota((BLOCK, 8), 0) // SPAN
    offset = jnp.zeros((BLOCK, 8), jnp.int32)
    for at, value in enumerate(OFFSETS):
        offset = jnp.where(o == at, sign * value, offset)
    target = me + offset
    target = jnp.where(target >= partitions, target - partitions, target)
    target = jnp.where(target < 0, target + partitions, target)
    chosen = jnp.where(peer == target, 1.0, 0.0)
    return dot(chosen, table)


def slot_columns(rows, block, width):
    slots = rows.shape[1]
    row = iota((BLOCK, slots), 0) % SPAN
    lane = iota((BLOCK, slots), 1)
    own = jnp.where(lane == row + block * SPAN, rows, 0.0)
    return dot(own, jnp.ones((slots, width), F32))


def edges(h, q, vx, vy, curve, opened, far, far_curve, width):
    layers = h.shape[0]
    curves = [curve[m * layers : (m + 1) * layers] for m in range(3)]
    sum_flow = jnp.zeros_like(h)
    sum_low = [jnp.zeros_like(h) for _ in range(3)]
    inflow = [jnp.zeros_like(h) for _ in range(3)]
    outflow = [jnp.zeros_like(h) for _ in range(3)]
    upper = list(q)
    lower = list(q)
    antis = []
    for j in range(6):
        cols = slice(j * width, (j + 1) * width)
        heading = j * math.pi / 3.0
        part = lambda i: far[i * layers : (i + 1) * layers, cols]
        op = opened[:, cols]
        along = math.cos(heading) * (vx + part(4))
        across = math.sin(heading) * (vy + part(5))
        u = op * (along + across) * 0.5 * ((h + part(3)) * 0.5)
        sum_flow = sum_flow + u
        up = jnp.maximum(u, 0.0)
        un = jnp.minimum(u, 0.0)
        ua = THIRD_ORDER * jnp.abs(u)
        row = []
        for m in range(3):
            qn = part(m)
            ln = far_curve[m * layers : (m + 1) * layers, cols]
            low = up * q[m] + un * qn
            high = u * (0.5 * (q[m] + qn) - (curves[m] + ln)) + ua * (ln - curves[m])
            sum_low[m] = sum_low[m] + low
            reached = jnp.where(op > 0, qn, q[m])
            upper[m] = jnp.maximum(upper[m], reached)
            lower[m] = jnp.minimum(lower[m], reached)
            a = high - low
            inflow[m] = inflow[m] + jnp.maximum(-a, 0.0)
            outflow[m] = outflow[m] + jnp.maximum(a, 0.0)
            row.append(a)
        antis.append(row)
    depth = h - sum_flow
    inverse = 1.0 / depth
    lowq, lim_in, lim_out = [], [], []
    for m in range(3):
        low = (h * q[m] - sum_low[m]) * inverse
        lowq.append(low)
        lim_in.append(jnp.minimum(1.0, (upper[m] - low) * depth / (inflow[m] + LIMIT_FLOOR)))
        lim_out.append(jnp.minimum(1.0, (low - lower[m]) * depth / (outflow[m] + LIMIT_FLOOR)))
    return depth, inverse, lowq, lim_in, lim_out, antis


def curvature(q, far_q, opened, width):
    layers = opened.shape[0]
    out = []
    for m in range(3):
        rows = slice(m * layers, (m + 1) * layers)
        total = jnp.zeros((layers, width), F32)
        for j in range(6):
            cols = slice(j * width, (j + 1) * width)
            total = total + opened[:, cols] * (far_q[rows, cols] - q[m])
        out.append(total * (1.0 / 12.0))
    return jnp.concatenate(out, axis=0)


def kernel(
    partitions,
    h_hbm,
    q_hbm,
    v_hbm,
    level_hbm,
    coc_hbm,
    peer_hbm,
    send_hbm,
    place_hbm,
    depth_ref,
    tracer_ref,
    h_ref,
    q_ref,
    v_ref,
    level_ref,
    coc_ref,
    peer_ref,
    send_ref,
    place_ref,
    load_sem,
    sent,
    came,
    table,
    g_own,
    g_b0,
    g_b1,
    far_own,
    far_b0,
    send_sem,
    recv_sem,
):
    layers, owned = h_ref.shape
    local = coc_ref.shape[1]
    halo = local - owned
    qrows = 3 * layers
    me = lax.axis_index("dom")
    targets = [lax.rem(me + (offset + partitions), partitions) for offset in OFFSETS]
    barrier = pltpu.get_barrier_semaphore()
    for target in targets:
        pl.semaphore_signal(
            barrier, inc=1, device_id={"dom": target}, device_id_type=pl.DeviceIdType.MESH
        )

    loads = [
        pltpu.make_async_copy(src, dst, load_sem.at[at])
        for at, (src, dst) in enumerate(
            (
                (peer_hbm, peer_ref),
                (send_hbm, send_ref),
                (q_hbm, q_ref),
                (h_hbm, h_ref),
                (v_hbm, v_ref),
                (place_hbm, place_ref),
                (coc_hbm, coc_ref),
                (level_hbm, level_ref),
            )
        )
    ]
    for load in loads:
        load.start()
    for load in loads[:5]:
        load.wait()

    peer = peer_ref[...]
    q = [q_ref[m] for m in range(3)]
    h = h_ref[...]
    vx = v_ref[0]
    vy = v_ref[1]
    fields = jnp.concatenate([q[0], q[1], q[2], h, vx, vy], axis=0)
    fields2 = pieces(fields)
    rows96 = 6 * layers
    blank = jnp.zeros((rows96, owned), BF16)
    edge = jnp.zeros((2 * layers, owned), BF16)
    edge1 = jnp.zeros((layers, owned), BF16)
    hi, lo = fields2[:rows96], fields2[rows96:]
    send_rows = peer_rows(peer, me, partitions, 1, send_ref[0].astype(F32))
    lane = iota((BLOCK, owned), 1).astype(F32)
    picks = [one_hot(slot_columns(send_rows, b, owned), lane) for b in range(3)]
    pay = []
    for b in range(2):
        total = None
        for piece in (hi, lo):
            main = jnp.concatenate([piece, edge], axis=0)
            if b == 0:
                tail = jnp.concatenate([blank, piece[: 2 * layers]], axis=0)
            else:
                tail = jnp.concatenate([blank, piece[2 * layers : qrows], edge1], axis=0)
            term = dot_nt(picks[b], main) + dot_nt(picks[2], tail)
            total = term if total is None else total + term
        pay.append(total)
    for p in range(8):
        sent[p, 0:SPAN] = pay[0][p * SPAN : (p + 1) * SPAN]
        sent[p, SPAN : 2 * SPAN] = pay[1][p * SPAN : (p + 1) * SPAN]
    pl.semaphore_wait(barrier, 8)
    copies = []
    for p in range(8):
        copy = pltpu.make_async_remote_copy(
            src_ref=sent.at[p],
            dst_ref=came.at[p],
            send_sem=send_sem.at[p],
            recv_sem=recv_sem.at[p],
            device_id={"dom": targets[p]},
            device_id_type=pl.DeviceIdType.MESH,
        )
        copy.start()
        copies.append(copy)

    for load in loads[5:]:
        load.wait()

    place_rows = peer_rows(peer, me, partitions, -1, (place_ref[0] - owned).astype(F32))
    keys = [slot_columns(place_rows, b, owned) for b in range(3)]
    keys = [jnp.where(key == float(halo), -4096.0, key) for key in keys]
    table[...] = jnp.zeros_like(table)
    table[0:6, 0:halo] = coc_ref[:, owned:local].astype(F32)
    table[8:9, 0:halo] = level_ref[:, owned:local].astype(F32)
    entries = table[...]
    above = jnp.where(entries >= float(owned), 1.0, 0.0)
    parts = jnp.concatenate([above, entries - above * float(owned)], axis=0).astype(BF16)
    width_t = table.shape[1]
    lane_t = iota((BLOCK, width_t), 1).astype(F32)
    found = []
    for b in range(3):
        got = dot_nt(parts, one_hot(keys[b][:, :width_t], lane_t))
        found.append(got[:16] * float(owned) + got[16:])
    own_idx = coc_ref[:, 0:owned].astype(F32)
    own_rows = iota((owned, owned), 0).astype(F32)
    for j in range(6):
        idx = own_idx[j : j + 1]
        cols = slice(j * owned, (j + 1) * owned)
        g_own[0:owned, cols] = one_hot(own_rows, idx)
        g_own[owned : owned + BLOCK, cols] = one_hot(keys[0], idx - float(owned))
        cols = slice(j * BLOCK, (j + 1) * BLOCK)
        idx = found[0][j : j + 1]
        g_b0[0:owned, cols] = one_hot(own_rows[:, :BLOCK], idx)
        for b in range(3):
            rows = slice(owned + b * BLOCK, owned + (b + 1) * BLOCK)
            g_b0[rows, cols] = one_hot(keys[b][:, :BLOCK], idx - float(owned))
        idx = found[1][j : j + 1]
        for b in range(3):
            rows = slice(b * BLOCK, (b + 1) * BLOCK)
            g_b1[rows, cols] = one_hot(keys[b][:, :BLOCK], idx - float(owned))

    lev_own = jnp.broadcast_to(level_ref[:, 0:owned].astype(F32), (layers, owned))
    lev_b = [jnp.broadcast_to(found[b][8:9], (layers, BLOCK)) for b in range(3)]
    lev_all = jnp.concatenate([lev_own] + lev_b, axis=1).astype(BF16)

    def opens(near, far, width):
        deep = jnp.concatenate([near] * 6, axis=1)
        layer = iota((layers, 6 * width), 0).astype(F32)
        return jnp.where(layer < jnp.minimum(deep, far), 1.0, 0.0)

    open_own = opens(lev_own, dot(lev_all[:, : owned + BLOCK], g_own[...]), owned)
    open_b0 = opens(lev_b[0], dot(lev_all, g_b0[...]), BLOCK)
    open_b1 = opens(lev_b[1], dot(lev_all[:, owned:], g_b1[...]), BLOCK)

    far_own[...] = joined(dot(fields2, g_own[0:owned, :]))
    far_b0[...] = joined(dot(fields2, g_b0[0:owned, :]))

    for copy in copies:
        copy.wait_recv()

    got0 = jnp.transpose(came[:, 0:SPAN, :].reshape(BLOCK, 8 * layers))
    got1 = jnp.transpose(came[:, SPAN : 2 * SPAN, :].reshape(BLOCK, 8 * layers))
    f0 = got0[:rows96]
    f1 = got1[:rows96]
    q2 = jnp.concatenate([got0[rows96:], got1[rows96 : rows96 + layers]], axis=0)
    fq = pieces(jnp.concatenate([f0[:qrows], f1[:qrows], q2], axis=1))
    fv = pieces(jnp.concatenate([f0[qrows:], f1[qrows:]], axis=1))
    far_o = far_own[...] + joined(dot(pieces(f0), g_own[owned : owned + BLOCK, :]))
    far_b0q = far_b0[0:qrows] + joined(dot(fq, g_b0[owned:, :]))
    far_b0v = far_b0[qrows:] + joined(dot(fv, g_b0[owned : owned + 2 * BLOCK, :]))
    far_b1q = dot(fq[:qrows], g_b1[...])

    def tracers_of(f):
        return [f[m * layers : (m + 1) * layers] for m in range(3)]

    q_b0 = tracers_of(f0)
    l_own = curvature(q, far_o, open_own, owned)
    l_b0 = curvature(q_b0, far_b0q, open_b0, BLOCK)
    l_b1 = curvature(tracers_of(f1), far_b1q, open_b1, BLOCK)
    l_all = jnp.concatenate([l_own, l_b0, l_b1], axis=1).astype(BF16)
    lfar_own = dot(l_all[:, : owned + BLOCK], g_own[...])
    lfar_b0 = dot(l_all, g_b0[0 : owned + 2 * BLOCK, :])

    far_b = jnp.concatenate([far_b0q, far_b0v], axis=0)
    h0, vx0, vy0 = (f0[i * layers : (i + 1) * layers] for i in range(3, 6))
    depth, inverse, lowq, lim_in, lim_out, antis = edges(
        h, q, vx, vy, l_own, open_own, far_o, lfar_own, owned
    )
    _, _, _, in0, out0, _ = edges(h0, q_b0, vx0, vy0, l_b0, open_b0, far_b, lfar_b0, BLOCK)
    lims = jnp.concatenate(
        [jnp.concatenate([a, b], axis=1) for a, b in zip(lim_in + lim_out, in0 + out0)], axis=0
    )
    rfar = dot(lims.astype(BF16), g_own[...])
    depth_ref[...] = depth
    for m in range(3):
        total = jnp.zeros_like(depth)
        for j in range(6):
            cols = slice(j * owned, (j + 1) * owned)
            a = antis[j][m]
            far_in = rfar[m * layers : (m + 1) * layers, cols]
            far_out = rfar[(3 + m) * layers : (4 + m) * layers, cols]
            factor = jnp.where(
                a > 0, jnp.minimum(lim_out[m], far_in), jnp.minimum(lim_in[m], far_out)
            )
            total = total + factor * a
        tracer_ref[m] = lowq[m] - total * inverse
    for copy in copies:
        copy.wait_send()


def store_kernel(depth_ref, tracer_ref, depth_hbm, tracer_hbm, sem):
    first = pltpu.make_async_copy(tracer_ref, tracer_hbm, sem.at[0])
    second = pltpu.make_async_copy(depth_ref, depth_hbm, sem.at[1])
    first.start()
    second.start()
    first.wait()
    second.wait()


def shards(
    partitions, thickness, tracers, velocity, max_level, cells_on_cell, peer_ids, send_ids, recv_pos
):
    layers, owned = thickness.shape
    args = (
        thickness,
        tracers,
        velocity,
        max_level.reshape(1, -1),
        cells_on_cell,
        peer_ids,
        send_ids,
        recv_pos,
    )
    args = tuple(pltpu.with_memory_space_constraint(arg, pltpu.HBM) for arg in args)
    outs = (
        jax.ShapeDtypeStruct(thickness.shape, F32),
        jax.ShapeDtypeStruct(tracers.shape, F32),
    )
    vmem = pl.BlockSpec(memory_space=pltpu.VMEM)
    hbm = pl.BlockSpec(memory_space=pltpu.HBM)
    results = pl.pallas_call(
        functools.partial(kernel, partitions),
        out_shape=tuple(pltpu.VMEM(out.shape, out.dtype) for out in outs),
        in_specs=[hbm] * 8,
        out_specs=[vmem] * 2,
        scratch_shapes=[pltpu.VMEM(arg.shape, arg.dtype) for arg in args]
        + [
            pltpu.SemaphoreType.DMA((8,)),
            pltpu.VMEM((8, 2 * SPAN, 8 * layers), F32),
            pltpu.VMEM((8, 2 * SPAN, 8 * layers), F32),
            pltpu.VMEM((16, owned), F32),
            pltpu.VMEM((owned + BLOCK, 6 * owned), BF16),
            pltpu.VMEM((owned + 3 * BLOCK, 6 * BLOCK), BF16),
            pltpu.VMEM((3 * BLOCK, 6 * BLOCK), BF16),
            pltpu.VMEM((6 * layers, 6 * owned), F32),
            pltpu.VMEM((6 * layers, 6 * BLOCK), F32),
            pltpu.SemaphoreType.DMA((8,)),
            pltpu.SemaphoreType.DMA((8,)),
        ],
        compiler_params=pltpu.CompilerParams(
            collective_id=0, has_side_effects=True, vmem_limit_bytes=40 * 1024 * 1024
        ),
    )(*args)
    results = [pltpu.with_memory_space_constraint(out, pltpu.VMEM) for out in results]
    return tuple(
        pl.pallas_call(
            store_kernel,
            out_shape=outs,
            in_specs=[vmem] * 2,
            out_specs=[hbm] * 2,
            scratch_shapes=[pltpu.SemaphoreType.DMA((2,))],
            compiler_params=pltpu.CompilerParams(vmem_limit_bytes=2 * 1024 * 1024),
        )(*results)
    )


def solution(mesh):
    return jax.shard_map(
        functools.partial(shards, mesh.shape["dom"]),
        mesh=mesh,
        in_specs=(
            P(None, ("groups", "dom")),
            P(None, None, ("groups", "dom")),
            P(None, None, ("groups", "dom")),
            P("dom"),
            P(None, "dom"),
            P("dom", None),
            P("dom", None, None),
            P("dom", None, None),
        ),
        out_specs=(P(None, ("groups", "dom")), P(None, None, ("groups", "dom"))),
        check_vma=False,
    )
```
